512 devices in a mesh: inner: 64 (over y, z), res: 8 (over x, core).
Axes of the slice: x: 4, y: 8, z: 8, core: 2. Of those that a mesh axis runs over, the one named last changes fastest.
Arguments:
- left_u: bfloat16 [8, 256, 1024, 64], P('res', 'inner'), may hold values from -6 to 6
- left_v: bfloat16 [8, 256, 1024, 64], P('res', 'inner'), may hold values from -0.1875 to 0.1875
- left_rank: int32 [8, 256], P('res', 'inner'), may hold values from 1 to 64
- right_u: bfloat16 [256, 8, 1024, 64], P('inner', 'res'), may hold values from -6 to 6
- right_v: bfloat16 [256, 8, 1024, 64], P('inner', 'res'), may hold values from -0.1875 to 0.1875
- right_rank: int32 [256, 8], P('inner', 'res'), may hold values from 1 to 64
- near_tiles: bfloat16 [64, 8, 1024, 1024], P('inner', 'res'), may hold values from -4 to 4
- near_block: int32 [64, 8], P('inner', 'res'), may hold values from -1 to 3
- comp_rank: int32 [8, 8], P(None, 'res'), may hold values from 16 to 64
- omega: bfloat16 [8, 1024, 64], P('res'), may hold values from -0.1875 to 0.1875
Outputs:
- basis: float32 [8, 8, 1024, 64], P(None, 'res', 'inner')
- image: float32 [8, 8, 1024, 64], P(None, 'res', 'inner')
The draws below stay inside these ranges and needn't reach their ends.
All inputs are finite; a program needn't handle non-finite values.
Results may differ from the reference program's by a relative error of at most 0.0059.
Values may be sent and summed in bfloat16 or wider, within the bound.
A program may use at most 64 MiB of HBM per device.

```python
import jax
import jax.numpy as jnp
from jax import lax

B = 1024
RMAX = 64
SR = 64
KB = 4
KT = 256
ROWS = 8
WCOLS = 8
SLOTS = 64


def set_ends(array, rng, smallest, top_value):
    dims = array.shape
    spot = [jax.random.randint(jax.random.fold_in(rng, axis), (), 0, dims[axis]) for axis in range(len(dims))]
    array = array.at[tuple(spot)].set(smallest)
    longest = dims.index(max(dims))
    spot[longest] = (spot[longest] + 1) % dims[longest]
    return array.at[tuple(spot)].set(top_value)


def level_of(rng, shape, split, low, top_value):
    def one(dim, shards_of):
        steps = jax.random.uniform(jax.random.fold_in(jax.random.fold_in(rng, 6), dim), (shards_of,), jnp.float32, low / len(split), top_value / len(split))
        return jnp.repeat(jnp.exp(steps), shape[dim] // shards_of).reshape((-1,) + (1,) * (len(shape) - dim - 1))

    factor_of = one(*split[0])
    for cut in split[1:]:
        factor_of = factor_of * one(*cut)
    return factor_of


def gaussian(key, shape, spread, reach, shards=(), held_as=jnp.bfloat16):
    drawn = jax.random.normal(key, shape, jnp.float32) * spread
    if len(shards) > 0:
        drawn = level_of(key, shape, shards, -0.22, 0.18) * drawn
    return jnp.clip(drawn, min=-reach, max=reach).astype(held_as)


def setup_inputs(seed: int = 0) -> dict:
    seeds = jax.random.split(jax.random.key(seed), 11)
    return {
        "left_u": gaussian(seeds[0], (ROWS, KT, B, RMAX), 1.0, 6.0, ((0, 8), (1, 64))),
        "left_v": gaussian(seeds[1], (ROWS, KT, B, RMAX), B ** -0.5, 0.1875, ((0, 8), (1, 64))),
        "left_rank": set_ends(jax.random.randint(seeds[2], (ROWS, KT), 1, RMAX + 1), jax.random.fold_in(seeds[2], 1), 1, RMAX).astype(jnp.int32),
        "right_u": gaussian(seeds[3], (KT, WCOLS, B, RMAX), 1.0, 6.0, ((0, 64), (1, 8))),
        "right_v": gaussian(seeds[4], (KT, WCOLS, B, RMAX), B ** -0.5, 0.1875, ((0, 64), (1, 8))),
        "right_rank": set_ends(jax.random.randint(seeds[5], (KT, WCOLS), 1, RMAX + 1), jax.random.fold_in(seeds[5], 1), 1, RMAX).astype(jnp.int32),
        "near_tiles": gaussian(seeds[6], (SLOTS, WCOLS, B, B), 0.3, 4.0, ((0, 64), (1, 8))),
        "near_block": set_ends(jax.random.randint(seeds[7], (SLOTS, WCOLS), -1, KB), jax.random.fold_in(seeds[7], 1), -1, KB - 1).astype(jnp.int32),
        "comp_rank": set_ends(jax.random.randint(seeds[8], (ROWS, WCOLS), SR // 4, SR + 1), jax.random.fold_in(seeds[8], 1), SR // 4, SR).astype(jnp.int32),
        "omega": gaussian(seeds[9], (WCOLS, B, SR), B ** -0.5, 0.1875, ((0, 8),)),
    }


def masked(factor, rank):
    columns = jnp.arange(factor.shape[-1])
    return factor * (columns < rank[..., None, None]).astype(factor.dtype)

def reference(left_u, left_v, left_rank, right_u, right_v, right_rank, near_tiles, near_block, comp_rank, omega):
    left_cut_u = masked(left_u, left_rank).astype(jnp.float32)
    left_cut_v = masked(left_v, left_rank).astype(jnp.float32)
    right_cut_u = masked(right_u, right_rank)
    right_cut_v = masked(right_v, right_rank)

    def column(inputs):
        col_u, col_v, col_near, col_block, col_comp, col_omega = inputs
        held = jnp.einsum('kbs,ikbr->iksr', col_u.astype(jnp.float32), left_cut_v).astype(jnp.bfloat16)
        far_part = jnp.einsum('kcs,iksr->ikcr', col_v.astype(jnp.float32), held.astype(jnp.float32)).astype(jnp.bfloat16)
        tile_index = (jnp.arange(SLOTS) * KB + jnp.maximum(col_block, 0)).astype(jnp.int32)
        near_rows = jnp.take(left_cut_v, tile_index, axis=1)
        near_part = jnp.einsum('pbc,ipbr->ipcr', col_near.astype(jnp.float32), near_rows).astype(jnp.bfloat16)
        is_near = (jnp.arange(KB)[None, :] == col_block[:, None]).reshape(KT)
        near_full = jnp.repeat(near_part, KB, axis=1)
        weight = jnp.where(is_near[None, :, None, None], near_full, far_part)
        active = (jnp.arange(SR)[None, :] < col_comp[:, None]).astype(jnp.float32)
        sketch_test = col_omega[None] * active[:, None, :].astype(jnp.bfloat16)
        expand = jnp.einsum('ikcr,ics->iksr', weight.astype(jnp.float32), sketch_test.astype(jnp.float32)).astype(jnp.bfloat16)
        sketch = jnp.einsum('ikbr,iksr->ibs', left_cut_u, expand.astype(jnp.float32))
        identity = jnp.eye(SR, dtype=sketch.dtype)
        gram = jnp.einsum('ibs,ibt->ist', sketch, sketch, precision=lax.Precision.HIGHEST)
        gram = gram + (1.0 - active).astype(sketch.dtype)[:, :, None] * identity
        lower_factor = jnp.linalg.cholesky(gram)
        basis = jnp.swapaxes(jax.scipy.linalg.solve_triangular(lower_factor, jnp.swapaxes(sketch, 1, 2), lower=True), 1, 2)
        basis_half = basis.astype(jnp.bfloat16)
        projected = jnp.einsum('ikbr,ibs->ikrs', left_cut_u, basis_half.astype(jnp.float32)).astype(jnp.bfloat16)
        images = jnp.einsum('ikcr,ikrs->ics', weight.astype(jnp.float32), projected.astype(jnp.float32))
        return (basis, images)
    inputs = (jnp.transpose(right_cut_u, (1, 0, 2, 3)), jnp.transpose(right_cut_v, (1, 0, 2, 3)), jnp.transpose(near_tiles, (1, 0, 2, 3)), near_block.T, comp_rank.T, omega)
    basis, images = lax.map(column, inputs)
    return (jnp.transpose(basis, (1, 0, 2, 3)), jnp.transpose(images, (1, 0, 2, 3)))
```

```python
import jax
import jax.numpy as jnp
from jax import lax
from jax.experimental import pallas as pl
from jax.experimental.pallas import tpu as pltpu
from jax.sharding import PartitionSpec as P

BF = jnp.bfloat16
F32 = jnp.float32
MESH = pl.DeviceIdType.MESH
HIGHEST = lax.Precision.HIGHEST
NY = 8
NZ = 8
NX = 4
COPIES = 160


def dot_nn(a, b, precision=None):
    return lax.dot_general(a, b, (((1,), (0,)), ((), ())), precision=precision, preferred_element_type=F32)


def dot_nt(a, b, precision=None):
    return lax.dot_general(a, b, (((1,), (1,)), ((), ())), precision=precision, preferred_element_type=F32)


def lanes(shape):
    return lax.broadcasted_iota(jnp.int32, shape, len(shape) - 1)


def row_mask(rank, shape):
    rows = lax.broadcasted_iota(jnp.int32, shape, 0)
    return jnp.where(rows < rank, 1.0, 0.0).astype(BF)


def inverse_factor(gram):
    lane32 = lanes((32, 128))
    rows32 = lax.broadcasted_iota(jnp.int32, (32, 128), 0)
    top = jnp.where(lane32 < 64, gram, jnp.where(lane32 - 64 == rows32, 1.0, 0.0))
    bottom = jnp.where(lane32 < 64, pltpu.roll(gram, 64, 1), jnp.where(lane32 - 96 == rows32, 1.0, 0.0))
    blocks = [top[8 * b : 8 * b + 8] for b in range(4)] + [bottom[8 * b : 8 * b + 8] for b in range(4)]
    rows8 = lax.broadcasted_iota(jnp.int32, (8, 128), 0)
    for k in range(64):
        kb, kr = k // 8, k % 8
        row = blocks[kb][kr : kr + 1, :]
        scaled = row / row[:, k : k + 1]
        for b in range(kb, 8):
            factor = blocks[b][:, k : k + 1]
            update = factor * scaled
            if b == kb:
                update = jnp.where(rows8 > kr, update, 0.0)
            blocks[b] = blocks[b] - update
    lane8 = lanes((8, 128))
    for b in range(8):
        diagonal = jnp.sum(jnp.where(lane8 == rows8 + 8 * b, blocks[b], 0.0), axis=1, keepdims=True)
        blocks[b] = blocks[b] * (1.0 / jnp.sqrt(diagonal))
    top = jnp.concatenate(blocks[:4], axis=0)
    bottom = jnp.concatenate(blocks[4:], axis=0)
    return jnp.where(lane32 < 64, pltpu.roll(top, 64, 1), bottom)


def block_pair(first, second):
    lane32 = lanes((32, 128))
    left = lane32 < 64
    return jnp.concatenate(
        [
            jnp.where(left, first, 0.0),
            jnp.where(left, pltpu.roll(first, 64, 1), 0.0),
            jnp.where(left, 0.0, pltpu.roll(second, 64, 1)),
            jnp.where(left, 0.0, second),
        ],
        axis=0,
    )


def kernel(
    lv_ref,
    lu_ref,
    ru_ref,
    rv_ref,
    near_ref,
    omega_ref,
    left_rank,
    right_rank,
    near_block,
    comp_rank,
    basis_ref,
    image_ref,
    lvb,
    wt,
    lum,
    rum,
    rvm,
    exs,
    exr,
    ska,
    skb,
    ra,
    rb,
    sa,
    sb,
    ra2,
    rb2,
    sfull,
    gs,
    gr,
    linvg,
    linvr,
    srr,
    ut,
    utr,
    lvsel,
    held,
    wgt,
    act,
    actr,
    ia,
    ib,
    imt,
    ria,
    rib,
    fa,
    fb,
    ria2,
    rib2,
    rows,
    send_sem,
    recv_sem,
):
    p = lax.axis_index("inner")
    r = lax.axis_index("res")
    y, z = p // NZ, p % NZ
    x, c = r // 2, r % 2
    used = [0]

    def at_y(d):
        return (lax.rem(y + d, NY) * NZ + z, r)

    def at_z(d):
        return (y * NZ + lax.rem(z + d, NZ), r)

    def at_res(q, par):
        return (p, lax.rem(x + q, NX) * 2 + (c if par == 0 else 1 - c))

    def res_of(q, par):
        return lax.rem(x + q, NX) * 2 + (c if par == 0 else 1 - c)

    def start(src, dst, device):
        n = used[0]
        used[0] += 1
        copy = pltpu.make_async_remote_copy(
            src_ref=src,
            dst_ref=dst,
            send_sem=send_sem.at[n],
            recv_sem=recv_sem.at[n],
            device_id=device,
            device_id_type=MESH,
        )
        copy.start()
        pending.append(copy)
        return copy

    pending = []
    pairs = [(q, par) for q in range(NX) for par in range(2)]
    others = pairs[1:]
    back = {(q, par): ((NX - q) % NX) * 2 + par for q, par in pairs}

    barrier = pltpu.get_barrier_semaphore()
    for d in range(1, NY):
        pl.semaphore_signal(barrier, inc=1, device_id=at_y(d), device_id_type=MESH)
    for d in range(1, NZ):
        pl.semaphore_signal(barrier, inc=1, device_id=at_z(d), device_id_type=MESH)
    for q, par in others:
        pl.semaphore_signal(barrier, inc=1, device_id=at_res(q, par), device_id_type=MESH)

    for k in range(4):
        lvb[k, 0, 0:64, :] = lv_ref[k] * row_mask(left_rank[0, k], (64, 1024))
    pl.semaphore_wait(barrier, NY - 1 + NZ - 1 + 7)

    own = [lvb.at[0:2, 0, 0:64], lvb.at[2:4, 0, 0:64]]
    sib_own = start(lvb.at[:, 0, 0:64], lvb.at[:, 0, 64:128], at_res(0, 1))
    from_left = [None, None]
    from_right = [None, None]
    from_left[0] = start(own[0], lvb.at[0:2, 3, 0:64], at_res(1, 0))
    from_right[1] = start(own[1], lvb.at[2:4, 1, 0:64], at_res(3, 0))
    from_left[1] = start(own[1], lvb.at[2:4, 3, 0:64], at_res(1, 0))
    from_right[0] = start(own[0], lvb.at[0:2, 1, 0:64], at_res(3, 0))

    act_came = []
    for q, par in pairs:
        lane8 = lanes((8, 128)) % 64
        unused = jnp.where(lane8 < comp_rank[res_of(q, par), 0], 0.0, 1.0)
        if (q, par) == (0, 0):
            actr[0] = unused
        else:
            act[2 * q + par] = unused
            act_came.append(start(act.at[2 * q + par], actr.at[back[(q, par)]], at_res(q, par)))

    nb = near_block[0, 0]
    for k in range(4):
        mask = row_mask(right_rank[k, 0], (64, 1024))
        rum[k] = ru_ref[k] * mask
        rvm[64 * k : 64 * k + 64, :] = rv_ref[k] * mask
        lum[64 * k : 64 * k + 64, :] = lu_ref[k] * row_mask(left_rank[0, k], (64, 1024))
    omega = omega_ref[...]
    mixed = [dot_nt(omega, rvm[64 * k : 64 * k + 64, :]) for k in range(4)]
    for n in range(4):
        cols = slice(256 * n, 256 * n + 256)
        near_omega = dot_nt(omega, near_ref[cols, :])
        for k in range(4):
            high = mixed[k].astype(BF)
            low = (mixed[k] - high.astype(F32)).astype(BF)
            part = dot_nn(high, rum[k, :, cols]) + dot_nn(low, rum[k, :, cols])
            full = jnp.where(nb == k, near_omega, part)
            high = full.astype(BF)
            wt[k, 0:64, cols] = high
            wt[k, 64:128, cols] = (full - high.astype(F32)).astype(BF)

    def expand_chip(q):
        lane = lanes((64, 128))
        parts = []
        for k in range(4):
            both = dot_nt(wt[k], lvb[k, q])
            parts.append(both[0:64] + both[64:128])
        rolled = [pltpu.roll(part, 64, 1) for part in parts]
        for par in range(2):
            if par == 0:
                tiles = [jnp.where(lane < 64, parts[2 * t], rolled[2 * t + 1]) for t in range(2)]
            else:
                tiles = [jnp.where(lane < 64, rolled[2 * t], parts[2 * t + 1]) for t in range(2)]
            active = row_mask(comp_rank[res_of(q, par), 0], (64, 128))
            for t in range(2):
                value = tiles[t].astype(BF) * active
                if (q, par) == (0, 0):
                    exr[0, :, 128 * t : 128 * t + 128] = value
                else:
                    exs[2 * q + par, :, 128 * t : 128 * t + 128] = value

    came = {}

    def send_expand(q, par):
        slot = back[(q, par)]
        came[slot] = start(exs.at[2 * q + par], exr.at[slot], at_res(q, par))

    sib_own.wait_recv()
    expand_chip(0)
    send_expand(0, 1)

    sibling = at_res(0, 1)
    fwd = {1: [], 2: [], 3: []}
    from_left[0].wait_recv()
    relay_left = start(lvb.at[0:2, 3, 0:64], lvb.at[0:2, 2, 0:64], at_res(1, 0))
    fwd[3].append(start(lvb.at[0:2, 3, 0:64], lvb.at[0:2, 3, 64:128], sibling))
    from_right[1].wait_recv()
    relay_right = start(lvb.at[2:4, 1, 0:64], lvb.at[2:4, 2, 0:64], at_res(3, 0))
    fwd[1].append(start(lvb.at[2:4, 1, 0:64], lvb.at[2:4, 1, 64:128], sibling))
    from_left[1].wait_recv()
    fwd[3].append(start(lvb.at[2:4, 3, 0:64], lvb.at[2:4, 3, 64:128], sibling))
    from_right[0].wait_recv()
    fwd[1].append(start(lvb.at[0:2, 1, 0:64], lvb.at[0:2, 1, 64:128], sibling))
    for q in (3, 1):
        for copy in fwd[q]:
            copy.wait_recv()
        expand_chip(q)
        send_expand(q, 0)
        send_expand(q, 1)
    relay_left.wait_recv()
    fwd[2].append(start(lvb.at[0:2, 2, 0:64], lvb.at[0:2, 2, 64:128], sibling))
    relay_right.wait_recv()
    fwd[2].append(start(lvb.at[2:4, 2, 0:64], lvb.at[2:4, 2, 64:128], sibling))
    for copy in fwd[2]:
        copy.wait_recv()
    expand_chip(2)
    send_expand(2, 0)
    send_expand(2, 1)

    for q in (0, 3, 1, 2):
        for par in range(2):
            if (q, par) != (0, 0):
                came[2 * q + par].wait_recv()
        factor = exr[2 * q : 2 * q + 2].reshape(128, 256)
        for n in range(4):
            part = dot_nn(factor, lum[:, 256 * n : 256 * n + 256]).astype(BF)
            for par in range(2):
                ska[2 * q + par, :, 256 * n : 256 * n + 256] = part[64 * par : 64 * par + 32]
                for t in range(2):
                    skb[2 * n + t, 2 * q + par] = part[64 * par + 32 : 64 * par + 64, 128 * t : 128 * t + 128]

    def slot_of(column):
        return lax.rem(column // 2 - x + NX, NX) * 2 + lax.rem(column + c, 2)

    got_a, got_b = [], []
    for d in range(1, 8):
        got_a.append(start(ska.at[slot_of(lax.rem(y + d, NY))], ra.at[d - 1], at_y(d)))
        got_b.append(start(skb.at[lax.rem(z + d, NZ)], rb.at[d - 1], at_z(d)))

    for k in range(4):
        for q in range(NX):
            kept = jnp.where(nb == k, lvb[k, q], lvsel[128 * q : 128 * q + 128, :] if k else jnp.zeros((128, 1024), BF))
            lvsel[128 * q : 128 * q + 128, :] = kept

    def weights(n, carry):
        cols = pl.ds(pl.multiple_of(n * 256, 256), 256)
        tile = near_ref[:, cols]
        for q in range(NX):
            near_part = dot_nn(lvsel[128 * q : 128 * q + 128, :], tile)
            for k in range(4):
                far_part = dot_nn(held[k, 128 * q : 128 * q + 128, 0:64], rvm[64 * k : 64 * k + 64, cols])
                value = jnp.where(nb == k, near_part, far_part).astype(BF)
                wgt[2 * q, 64 * k : 64 * k + 64, cols] = value[0:64]
                wgt[2 * q + 1, 64 * k : 64 * k + 64, cols] = value[64:128]
        return carry

    for k in range(4):
        for q in range(NX):
            held[k, 128 * q : 128 * q + 128, 0:64] = dot_nt(lvb[k, q], rum[k]).astype(BF)
    lax.fori_loop(0, 4, weights, 0)

    for copy in got_a:
        copy.wait_recv()
    mine = slot_of(y)
    for n in range(8):
        cols = slice(128 * n, 128 * n + 128)
        total = ska[mine, :, cols].astype(F32)
        for d in range(7):
            total = total + ra[d, :, cols].astype(F32)
        sa[n] = total
    got_a = [start(sa.at[lax.rem(z + d, NZ)], ra2.at[d - 1], at_z(d)) for d in range(1, 8)]
    for copy in got_b:
        copy.wait_recv()
    for n in range(8):
        total = skb[z, n].astype(F32)
        for d in range(7):
            total = total + rb[d, n].astype(F32)
        sb[n] = total
    got_b = [start(sb.at[slot_of(lax.rem(y + d, NY))], rb2.at[d - 1], at_y(d)) for d in range(1, 8)]
    for copy in got_a + got_b:
        copy.wait_recv()
    low_half = sa[z]
    high_half = sb[mine]
    for d in range(7):
        low_half = low_half + ra2[d]
        high_half = high_half + rb2[d]

    zcols = pl.ds(pl.multiple_of(z * 128, 128), 128)
    sfull[y, 0:32, zcols] = low_half.astype(BF)
    sfull[y, 32:64, zcols] = high_half.astype(BF)
    got_a, got_b = [], []
    for d in range(1, 8):
        got_a.append(start(sfull.at[y, 0:32, zcols], sfull.at[y, 0:32, zcols], at_z(d)))
        got_b.append(start(sfull.at[y, 32:64, zcols], sfull.at[y, 32:64, zcols], at_y(d)))

    part = jnp.concatenate([low_half, high_half], axis=0)
    twice = jnp.concatenate([part, part], axis=0)
    gram = dot_nt(part, twice, HIGHEST)
    gs[...] = jnp.where(lanes((32, 128)) < 64, gram[0:32], gram[32:64])
    got_gram = [start(gs, gr.at[d - 1], at_z(d)) for d in range(1, 8)]

    for copy in got_a:
        copy.wait_recv()
    got_a = [start(sfull.at[y, 0:32], sfull.at[y, 0:32], at_y(d)) for d in range(1, 8)]
    for copy in got_b:
        copy.wait_recv()
    got_b = [start(sfull.at[:, 32:64, zcols], sfull.at[:, 32:64, zcols], at_z(d)) for d in range(1, 8)]

    for copy in got_gram:
        copy.wait_recv()
    total = gs[...]
    for d in range(7):
        total = total + gr[d]
    lane32 = lanes((32, 128))
    rows32 = lax.broadcasted_iota(jnp.int32, (32, 128), 0)
    index = jnp.where(lane32 < 64, rows32, rows32 + 32)
    for copy in act_came:
        copy.wait_recv()
    unused = jnp.where(lane32 % 64 == index, actr[mine, 0:1, :], 0.0)
    linvg[y] = inverse_factor(total + unused)
    got_inverse = [start(linvg.at[y], linvg.at[y], at_y(d)) for d in range(1, 8)]

    for copy in got_a + got_b:
        copy.wait_recv()

    for j in range(0, 8, 2):
        value = dot_nt(sfull[j : j + 2].reshape(128, 1024), lum[...]).astype(BF)
        ut[j] = value[0:64]
        ut[j + 1] = value[64:128]
    came = {}
    for q, par in others:
        came[back[(q, par)]] = start(ut.at[res_of(q, par)], utr.at[back[(q, par)]], at_res(q, par))
    utr[0] = ut[r]
    row_cols = pl.ds(pl.multiple_of(y * 128, 128), 128)
    rows_came = []
    for q, par in others:
        rows_came.append(start(sfull.at[res_of(q, par), :, row_cols], srr.at[back[(q, par)]], at_res(q, par)))
    srr[0] = sfull[r, :, row_cols]
    for copy in got_inverse:
        copy.wait_recv()
    inverse_came = []
    for q, par in others:
        inverse_came.append(start(linvg.at[res_of(q, par)], linvr.at[back[(q, par)]], at_res(q, par)))
    linvr[0] = linvg[r]

    got_a, got_b = [], []
    for slot in (0, 1, 6, 7, 2, 3, 4, 5):
        if slot:
            came[slot].wait_recv()
        factor = utr[slot]
        for n in range(4):
            part = dot_nn(factor, wgt[slot, :, 256 * n : 256 * n + 256])
            for t in range(2):
                tile = part[:, 128 * t : 128 * t + 128]
                if slot < 4:
                    ia[2 * n + t, 64 * slot : 64 * slot + 64, :] = tile.astype(BF)
                else:
                    imt[2 * n + t, 64 * (slot - 4) : 64 * (slot - 4) + 64, :] = tile
        if slot == 3:
            for d in range(1, 8):
                got_a.append(start(ia.at[lax.rem(y + d, NY)], ria.at[d - 1], at_y(d)))
    for n in range(8):
        ib[:, n] = imt[n].T.astype(BF).reshape(8, 16, 256)
    for d in range(1, 8):
        got_b.append(start(ib.at[lax.rem(z + d, NZ)], rib.at[d - 1], at_z(d)))

    for copy in got_a:
        copy.wait_recv()
    total = ia[y].astype(F32)
    for d in range(7):
        total = total + ria[d].astype(F32)
    fa[...] = total.T.reshape(8, 16, 256)
    got_a = [start(fa.at[lax.rem(z + d, NZ)], ria2.at[d - 1], at_z(d)) for d in range(1, 8)]
    for copy in got_b:
        copy.wait_recv()
    for n in range(8):
        total = ib[z, n].astype(F32)
        for d in range(7):
            total = total + rib[d, n].astype(F32)
        fb[n] = total
    got_b = [start(fb.at[lax.rem(y + d, NY)], rib2.at[d - 1], at_y(d)) for d in range(1, 8)]

    for copy in rows_came + inverse_came:
        copy.wait_recv()
    both = []
    for t in range(NX):
        factor = block_pair(linvr[2 * t], linvr[2 * t + 1])
        both.append(factor)
        turned = dot_nn(factor, srr[2 * t : 2 * t + 2].reshape(128, 128).astype(F32), HIGHEST).T
        rows[...] = turned.reshape(8, 16, 128)
        value = rows[z]
        basis_ref[res_of(t, 0)] = value[:, 0:64]
        basis_ref[res_of(t, 1)] = pltpu.roll(value, 64, 1)[:, 0:64]
    for copy in got_a + got_b:
        copy.wait_recv()
    first, second = fa[z], fb[y]
    for d in range(7):
        first = first + ria2[d]
        second = second + rib2[d]
    for t in range(NX):
        half = first if t < 2 else second
        value = dot_nt(half[:, 128 * (t % 2) : 128 * (t % 2) + 128], both[t], HIGHEST)
        image_ref[res_of(t, 0)] = value[:, 0:64]
        image_ref[res_of(t, 1)] = pltpu.roll(value, 64, 1)[:, 0:64]
    for copy in pending:
        copy.wait_send()


def local(
    left_u,
    left_v,
    left_rank,
    right_u,
    right_v,
    right_rank,
    near_tiles,
    near_block,
    comp_rank,
    omega,
):
    vmem = pl.BlockSpec(memory_space=pltpu.VMEM)
    smem = pl.BlockSpec(memory_space=pltpu.SMEM)
    scratch = [
        ((4, 4, 128, 1024), BF),
        ((4, 128, 1024), BF),
        ((256, 1024), BF),
        ((4, 64, 1024), BF),
        ((256, 1024), BF),
        ((8, 64, 256), BF),
        ((8, 64, 256), BF),
        ((8, 32, 1024), BF),
        ((8, 8, 32, 128), BF),
        ((7, 32, 1024), BF),
        ((7, 8, 32, 128), BF),
        ((8, 32, 128), F32),
        ((8, 32, 128), F32),
        ((7, 32, 128), F32),
        ((7, 32, 128), F32),
        ((8, 64, 1024), BF),
        ((32, 128), F32),
        ((7, 32, 128), F32),
        ((8, 32, 128), F32),
        ((8, 32, 128), F32),
        ((8, 64, 128), BF),
        ((8, 64, 256), BF),
        ((8, 64, 256), BF),
        ((512, 1024), BF),
        ((4, 512, 64), BF),
        ((8, 256, 1024), BF),
        ((8, 8, 128), F32),
        ((8, 8, 128), F32),
        ((8, 256, 128), BF),
        ((8, 8, 16, 256), BF),
        ((8, 256, 128), F32),
        ((7, 256, 128), BF),
        ((7, 8, 16, 256), BF),
        ((8, 16, 256), F32),
        ((8, 16, 256), F32),
        ((7, 16, 256), F32),
        ((7, 16, 256), F32),
        ((8, 16, 128), F32),
    ]
    basis, image = pl.pallas_call(
        kernel,
        out_shape=[jax.ShapeDtypeStruct((8, 16, 64), F32)] * 2,
        in_specs=[vmem] * 6 + [smem] * 4,
        out_specs=[vmem, vmem],
        scratch_shapes=[pltpu.VMEM(shape, dtype) for shape, dtype in scratch]
        + [pltpu.SemaphoreType.DMA((COPIES,)), pltpu.SemaphoreType.DMA((COPIES,))],
        compiler_params=pltpu.CompilerParams(
            collective_id=0, has_side_effects=True, vmem_limit_bytes=50 * 1024 * 1024
        ),
    )(
        jnp.swapaxes(left_v[0], 1, 2),
        jnp.swapaxes(left_u[0], 1, 2),
        jnp.swapaxes(right_u[:, 0], 1, 2),
        jnp.swapaxes(right_v[:, 0], 1, 2),
        near_tiles[0, 0],
        jnp.swapaxes(omega[0], 0, 1),
        left_rank,
        right_rank,
        near_block,
        comp_rank,
    )
    return basis[:, None], image[:, None]


def solution(mesh):
    placed = (
        P("res", "inner", None, None),
        P("res", "inner", None, None),
        P("res", "inner"),
        P("inner", "res", None, None),
        P("inner", "res", None, None),
        P("inner", "res"),
        P("inner", "res", None, None),
        P("inner", "res"),
        P(None, "res"),
        P("res", None, None),
    )
    return jax.shard_map(
        local,
        mesh=mesh,
        in_specs=placed,
        out_specs=(P(None, "res", "inner", None), P(None, "res", "inner", None)),
        check_vma=False,
    )
```

```python
import jax
import jax.numpy as jnp
from jax import lax
from jax.experimental import pallas as pl
from jax.experimental.pallas import tpu as pltpu
from jax.sharding import PartitionSpec as P

BF = jnp.bfloat16
F32 = jnp.float32
MESH = pl.DeviceIdType.MESH
HIGHEST = lax.Precision.HIGHEST
NY = 8
NZ = 8
NX = 4
COPIES = 180


def dot_nn(a, b, precision=None):
    return lax.dot_general(a, b, (((1,), (0,)), ((), ())), precision=precision, preferred_element_type=F32)


def dot_nt(a, b, precision=None):
    return lax.dot_general(a, b, (((1,), (1,)), ((), ())), precision=precision, preferred_element_type=F32)


def lanes(shape):
    return lax.broadcasted_iota(jnp.int32, shape, len(shape) - 1)


def row_mask(rank, shape):
    rows = lax.broadcasted_iota(jnp.int32, shape, 0)
    return jnp.where(rows < rank, 1.0, 0.0).astype(BF)


def unpack_with_identity(gram):
    lane32 = lanes((32, 128))
    rows32 = lax.broadcasted_iota(jnp.int32, (32, 128), 0)
    top = jnp.where(lane32 < 64, gram, jnp.where(lane32 - 64 == rows32, 1.0, 0.0))
    bottom = jnp.where(lane32 < 64, pltpu.roll(gram, 64, 1), jnp.where(lane32 - 96 == rows32, 1.0, 0.0))
    return [top[8 * b : 8 * b + 8] for b in range(4)] + [bottom[8 * b : 8 * b + 8] for b in range(4)]


def eliminate(blocks, first, last):
    rows8 = lax.broadcasted_iota(jnp.int32, (8, 128), 0)
    for k in range(first, last):
        kb, kr = k // 8, k % 8
        row = blocks[kb][kr : kr + 1, :]
        scaled = row / row[:, k : k + 1]
        for b in range(kb, 8):
            update = blocks[b][:, k : k + 1] * scaled
            if b == kb:
                update = jnp.where(rows8 > kr, update, 0.0)
            blocks[b] = blocks[b] - update


def inverse_of(blocks):
    lane8 = lanes((8, 128))
    lane32 = lanes((32, 128))
    rows8 = lax.broadcasted_iota(jnp.int32, (8, 128), 0)
    scaled = []
    for b in range(8):
        diagonal = jnp.sum(jnp.where(lane8 == rows8 + 8 * b, blocks[b], 0.0), axis=1, keepdims=True)
        scaled.append(blocks[b] * (1.0 / jnp.sqrt(diagonal)))
    top = jnp.concatenate(scaled[:4], axis=0)
    bottom = jnp.concatenate(scaled[4:], axis=0)
    return jnp.where(lane32 < 64, pltpu.roll(top, 64, 1), bottom)


def block_pair(first, second):
    lane32 = lanes((32, 128))
    left = lane32 < 64
    return jnp.concatenate(
        [
            jnp.where(left, first, 0.0),
            jnp.where(left, pltpu.roll(first, 64, 1), 0.0),
            jnp.where(left, 0.0, pltpu.roll(second, 64, 1)),
            jnp.where(left, 0.0, second),
        ],
        axis=0,
    )


def kernel(
    lv_hbm,
    lu_hbm,
    ru_hbm,
    rv_hbm,
    near_hbm,
    omega_hbm,
    left_rank,
    right_rank,
    near_block,
    comp_rank,
    basis_ref,
    image_ref,
    lv_ref,
    lu_ref,
    ru_ref,
    rv_ref,
    near_ref,
    omega_ref,
    lvb,
    wt,
    lum,
    rum,
    rvm,
    exs,
    exr,
    ska,
    skb,
    ra,
    rb,
    sa,
    sb,
    ra2,
    rb2,
    sfull,
    gs,
    gr,
    linvg,
    linvr,
    srr,
    ut,
    utr,
    lvsel,
    held,
    wgt,
    act,
    actr,
    ia,
    ib,
    ria,
    rib,
    fa,
    fb,
    ria2,
    rib2,
    rows,
    load_sem,
    send_sem,
    recv_sem,
):
    p = lax.axis_index("inner")
    r = lax.axis_index("res")
    y, z = p // NZ, p % NZ
    x, c = r // 2, r % 2
    used = [0]
    moves = (
        (lv_hbm, lv_ref),
        (rv_hbm, rv_ref),
        (omega_hbm, omega_ref),
        (ru_hbm, ru_ref),
        (near_hbm, near_ref),
        (lu_hbm, lu_ref),
    )
    loads = [pltpu.make_async_copy(src, dst, load_sem.at[n]) for n, (src, dst) in enumerate(moves)]
    for load in loads:
        load.start()

    def at_y(d):
        return (lax.rem(y + d, NY) * NZ + z, r)

    def at_z(d):
        return (y * NZ + lax.rem(z + d, NZ), r)

    def at_res(q, par):
        return (p, lax.rem(x + q, NX) * 2 + (c if par == 0 else 1 - c))

    def res_of(q, par):
        return lax.rem(x + q, NX) * 2 + (c if par == 0 else 1 - c)

    def start(src, dst, device):
        n = used[0]
        used[0] += 1
        copy = pltpu.make_async_remote_copy(
            src_ref=src,
            dst_ref=dst,
            send_sem=send_sem.at[n],
            recv_sem=recv_sem.at[n],
            device_id=device,
            device_id_type=MESH,
        )
        copy.start()
        pending.append(copy)
        return copy

    pending = []

    def start_unless_own(distance, src, lands, base, device):
        n = lax.rem(distance + 7, 8)

        @pl.when(distance != 0)
        def _():
            pltpu.make_async_remote_copy(
                src_ref=src,
                dst_ref=lands.at[n],
                send_sem=send_sem.at[base + n],
                recv_sem=recv_sem.at[base + n],
                device_id=device,
                device_id_type=MESH,
            ).start()

    pairs = [(q, par) for q in range(NX) for par in range(2)]
    others = pairs[1:]
    back = {(q, par): ((NX - q) % NX) * 2 + par for q, par in pairs}

    barrier = pltpu.get_barrier_semaphore()
    for d in range(1, NY):
        pl.semaphore_signal(barrier, inc=1, device_id=at_y(d), device_id_type=MESH)
    for d in range(1, NZ):
        pl.semaphore_signal(barrier, inc=1, device_id=at_z(d), device_id_type=MESH)
    for q, par in others:
        pl.semaphore_signal(barrier, inc=1, device_id=at_res(q, par), device_id_type=MESH)

    loads[0].wait()
    for k in range(4):
        lvb[k, 0, 0:64, :] = lv_ref[k] * row_mask(left_rank[0, k], (64, 1024))
    pl.semaphore_wait(barrier, NY - 1 + NZ - 1 + 7)

    nb = near_block[0, 0]

    def pick_near(q):
        rows = slice(128 * q, 128 * q + 128)
        kept = jnp.zeros((128, 1024), BF)
        for k in range(4):
            kept = jnp.where(nb == k, lvb[k, q], kept)
            held[k, rows, :] = dot_nt(lvb[k, q], rum[k]).astype(BF)
        lvsel[rows, :] = kept

    def make_weights(n):
        cols = slice(256 * n, 256 * n + 256)
        tile = near_ref[:, cols]
        for q in range(NX):
            rows = slice(128 * q, 128 * q + 128)
            near_part = dot_nn(lvsel[rows, :], tile)
            for k in range(4):
                far_part = dot_nn(held[k, rows, :], rvm[64 * k : 64 * k + 64, cols])
                value = jnp.where(nb == k, near_part, far_part).astype(BF)
                wgt[2 * q, 64 * k : 64 * k + 64, cols] = value[0:64]
                wgt[2 * q + 1, 64 * k : 64 * k + 64, cols] = value[64:128]

    def piece_of(step, n):
        return lambda: step(n)

    weight_work = [piece_of(pick_near, q) for q in range(4)] + [piece_of(make_weights, n) for n in range(4)]

    halves = (slice(0, 2), slice(2, 4))
    sibling = at_res(0, 1)
    sib_own = start(lvb.at[:, 0, 0:64], lvb.at[:, 0, 64:128], sibling)
    came_v = {}
    for half in halves:
        came_v[3, half.start] = start(lvb.at[half, 0, 0:64], lvb.at[half, 3, 0:64], at_res(1, 0))
        came_v[1, half.start] = start(lvb.at[half, 0, 0:64], lvb.at[half, 1, 0:64], at_res(3, 0))

    act_came = []
    for q, par in pairs:
        lane8 = lanes((8, 128)) % 64
        unused = jnp.where(lane8 < comp_rank[0, res_of(q, par)], 0.0, 1.0)
        if (q, par) == (0, 0):
            actr[0] = unused
        else:
            act[2 * q + par] = unused
            act_came.append(start(act.at[2 * q + par], actr.at[back[(q, par)]], at_res(q, par)))

    for load in loads[1:]:
        load.wait()
    for k in range(4):
        mask = row_mask(right_rank[0, k], (64, 1024))
        rum[k] = ru_ref[k] * mask
        rvm[64 * k : 64 * k + 64, :] = rv_ref[k] * mask
        lum[64 * k : 64 * k + 64, :] = lu_ref[k] * row_mask(left_rank[0, k], (64, 1024))
    omega = omega_ref[...]
    mixed = [dot_nt(omega, rvm[64 * k : 64 * k + 64, :]) for k in range(4)]
    for n in range(4):
        cols = slice(256 * n, 256 * n + 256)
        near_omega = dot_nt(omega, near_ref[cols, :])
        for k in range(4):
            high = mixed[k].astype(BF)
            low = (mixed[k] - high.astype(F32)).astype(BF)
            part = dot_nn(high, rum[k, :, cols]) + dot_nn(low, rum[k, :, cols])
            full = jnp.where(nb == k, near_omega, part)
            high = full.astype(BF)
            wt[k, 0:64, cols] = high
            wt[k, 64:128, cols] = (full - high.astype(F32)).astype(BF)

    def expand_chip(q):
        lane = lanes((64, 128))
        parts = []
        for k in range(4):
            both = dot_nt(wt[k], lvb[k, q])
            parts.append(both[0:64] + both[64:128])
        rolled = [pltpu.roll(part, 64, 1) for part in parts]
        for par in range(2):
            if par == 0:
                tiles = [jnp.where(lane < 64, parts[2 * t], rolled[2 * t + 1]) for t in range(2)]
            else:
                tiles = [jnp.where(lane < 64, rolled[2 * t], parts[2 * t + 1]) for t in range(2)]
            active = row_mask(comp_rank[0, res_of(q, par)], (64, 128))
            for t in range(2):
                value = tiles[t].astype(BF) * active
                if (q, par) == (0, 0):
                    exr[0, :, 128 * t : 128 * t + 128] = value
                else:
                    exs[2 * q + par, :, 128 * t : 128 * t + 128] = value

    came = {}

    def send_expand(q, par):
        slot = back[(q, par)]
        came[slot] = start(exs.at[2 * q + par], exr.at[slot], at_res(q, par))

    for half in halves:
        came_v[2, half.start] = start(lvb.at[half, 0, 0:64], lvb.at[half, 2, 0:64], at_res(2, 0))
    sib_own.wait_recv()
    expand_chip(0)
    send_expand(0, 1)

    fwd = {1: [], 2: [], 3: []}

    def forward(q, half):
        came_v[q, half.start].wait_recv()
        fwd[q].append(start(lvb.at[half, q, 0:64], lvb.at[half, q, 64:128], sibling))

    def expand_and_send(q):
        for copy in fwd[q]:
            copy.wait_recv()
        expand_chip(q)
        send_expand(q, 0)
        send_expand(q, 1)

    def slot_of(column):
        return lax.rem(column // 2 - x + NX, NX) * 2 + lax.rem(column + c, 2)

    place = {0: 0, 3: 1, 1: 2, 2: 3}

    def sketch_chip(q):
        for par in range(2):
            if (q, par) != (0, 0):
                came[2 * q + par].wait_recv()
        factor = exr[2 * q : 2 * q + 2].reshape(128, 256)
        for n in range(4):
            part = dot_nn(factor, lum[:, 256 * n : 256 * n + 256]).astype(BF)
            for par in range(2):
                ska[2 * q + par, :, 256 * n : 256 * n + 256] = part[64 * par : 64 * par + 32]
                for t in range(2):
                    tile = part[64 * par + 32 : 64 * par + 64, 128 * t : 128 * t + 128]
                    skb[2 * n + t, 2 * place[q] + par] = tile
        for par in range(2):
            column = res_of(q, par)
            distance = lax.rem(column - y + NY, NY)
            start_unless_own(distance, ska.at[2 * q + par], ra, sums_base, (column * NZ + z, r))

    got_b = []

    def send_high(tiles):
        for d in range(1, NZ):
            got_b.append(start(skb.at[lax.rem(z + d, NZ), tiles], rb.at[d - 1, tiles], at_z(d)))

    sums_base = used[0]
    used[0] += 7
    got_a = []
    for d in range(7):
        got_a.append(
            pltpu.make_async_remote_copy(
                src_ref=ska.at[0],
                dst_ref=ra.at[d],
                send_sem=send_sem.at[sums_base + d],
                recv_sem=recv_sem.at[sums_base + d],
                device_id=at_y(d + 1),
                device_id_type=MESH,
            )
        )
    pending.extend(got_a)
    for half in halves:
        forward(3, half)
        forward(1, half)
    expand_and_send(3)
    expand_and_send(1)
    sketch_chip(0)
    for half in halves:
        forward(2, half)
    expand_and_send(2)
    sketch_chip(3)
    sketch_chip(1)
    send_high(slice(0, 6))
    sketch_chip(2)
    send_high(slice(6, 8))
    for piece in weight_work:
        piece()
    for copy in got_a:
        copy.wait_recv()
    mine = slot_of(y)
    for n in range(8):
        cols = slice(128 * n, 128 * n + 128)
        total = ska[mine, :, cols].astype(F32)
        for d in range(7):
            total = total + ra[d, :, cols].astype(F32)
        sa[n] = total
    got_a = [start(sa.at[lax.rem(z + d, NZ)], ra2.at[d - 1], at_z(d)) for d in range(1, 8)]
    for copy in got_b:
        copy.wait_recv()
    for q, par in pairs:
        n = 2 * place[q] + par
        total = skb[z, n].astype(F32)
        for d in range(7):
            total = total + rb[d, n].astype(F32)
        sb[2 * q + par] = total
    got_b = [start(sb.at[slot_of(lax.rem(y + d, NY))], rb2.at[d - 1], at_y(d)) for d in range(1, 8)]
    for copy in got_a + got_b:
        copy.wait_recv()
    low_half = sa[z]
    high_half = sb[mine]
    for d in range(7):
        low_half = low_half + ra2[d]
        high_half = high_half + rb2[d]

    zcols = pl.ds(pl.multiple_of(z * 128, 128), 128)
    sfull[y, 0:32, zcols] = low_half.astype(BF)
    sfull[y, 32:64, zcols] = high_half.astype(BF)
    got_a, got_b = [], []
    for d in range(1, 8):
        got_a.append(start(sfull.at[y, 0:32, zcols], sfull.at[y, 0:32, zcols], at_z(d)))
        got_b.append(start(sfull.at[y, 32:64, zcols], sfull.at[y, 32:64, zcols], at_y(d)))

    part = jnp.concatenate([low_half, high_half], axis=0)
    twice = jnp.concatenate([part, part], axis=0)
    gram = dot_nt(part, twice, HIGHEST)
    gs[...] = jnp.where(lanes((32, 128)) < 64, gram[0:32], gram[32:64])
    got_gram = [start(gs, gr.at[d - 1], at_z(d)) for d in range(1, 8)]

    for copy in got_a:
        copy.wait_recv()
    spread = [start(sfull.at[y, 0:32], sfull.at[y, 0:32], at_y(d)) for d in range(1, 8)]
    for copy in got_b:
        copy.wait_recv()
    spread += [start(sfull.at[:, 32:64, zcols], sfull.at[:, 32:64, zcols], at_z(d)) for d in range(1, 8)]

    blocks = []

    def sum_gram():
        for copy in got_gram + act_came:
            copy.wait_recv()
        total = gs[...]
        for d in range(7):
            total = total + gr[d]
        lane32 = lanes((32, 128))
        rows32 = lax.broadcasted_iota(jnp.int32, (32, 128), 0)
        index = jnp.where(lane32 < 64, rows32, rows32 + 32)
        unused = jnp.where(lane32 % 64 == index, actr[mine, 0:1, :], 0.0)
        blocks.extend(unpack_with_identity(total + unused))

    sum_gram()
    eliminate(blocks, 0, 40)
    for copy in spread:
        copy.wait_recv()

    for j in range(0, 8, 2):
        value = dot_nt(sfull[j : j + 2].reshape(128, 1024), lum[...]).astype(BF)
        ut[j] = value[0:64]
        ut[j + 1] = value[64:128]
    came = {}
    for q, par in others:
        came[back[(q, par)]] = start(ut.at[res_of(q, par)], utr.at[back[(q, par)]], at_res(q, par))
    utr[0] = ut[r]
    row_cols = pl.ds(pl.multiple_of(y * 128, 128), 128)
    rows_came = []
    for q, par in others:
        rows_came.append(start(sfull.at[res_of(q, par), :, row_cols], srr.at[back[(q, par)]], at_res(q, par)))
    srr[0] = sfull[r, :, row_cols]
    eliminate(blocks, 40, 64)
    linvg[y] = inverse_of(blocks)
    got_inverse = [start(linvg.at[y], linvg.at[y], at_y(d)) for d in range(1, 8)]

    for slot in range(4):
        if slot:
            came[slot].wait_recv()
        for n in range(4):
            part = dot_nn(utr[slot], wgt[slot, :, 256 * n : 256 * n + 256])
            for t in range(2):
                tile = part[:, 128 * t : 128 * t + 128]
                ia[2 * n + t, 64 * slot : 64 * slot + 64, :] = tile.astype(BF)
    got_a = [start(ia.at[lax.rem(y + d, NY)], ria.at[d - 1], at_y(d)) for d in range(1, 8)]
    for pair in (1, 0):
        slot = 4 + 2 * pair
        came[slot].wait_recv()
        came[slot + 1].wait_recv()
        for n in range(4):
            cols = slice(256 * n, 256 * n + 256)
            part = jnp.concatenate(
                [dot_nn(utr[slot], wgt[slot, :, cols]), dot_nn(utr[slot + 1], wgt[slot + 1, :, cols])], axis=0
            )
            for t in range(2):
                turned = part[:, 128 * t : 128 * t + 128].T.astype(BF)
                ib[:, 2 * n + t, :, 128 * pair : 128 * pair + 128] = turned.reshape(8, 16, 128)
    got_b = [start(ib.at[lax.rem(z + d, NZ)], rib.at[d - 1], at_z(d)) for d in range(1, 8)]
    for copy in got_inverse:
        copy.wait_recv()
    inverse_came = []
    for q, par in others:
        inverse_came.append(start(linvg.at[res_of(q, par)], linvr.at[back[(q, par)]], at_res(q, par)))
    linvr[0] = linvg[r]
    for copy in got_a:
        copy.wait_recv()
    total = ia[y].astype(F32)
    for d in range(7):
        total = total + ria[d].astype(F32)
    fa[...] = total.T.reshape(8, 16, 256)
    got_a = [start(fa.at[lax.rem(z + d, NZ)], ria2.at[d - 1], at_z(d)) for d in range(1, 8)]
    for copy in got_b:
        copy.wait_recv()
    for n in range(8):
        total = ib[z, n].astype(F32)
        for d in range(7):
            total = total + rib[d, n].astype(F32)
        fb[n] = total
    got_b = [start(fb.at[lax.rem(y + d, NY)], rib2.at[d - 1], at_y(d)) for d in range(1, 8)]

    for copy in rows_came + inverse_came:
        copy.wait_recv()
    both = []
    for t in range(NX):
        factor = block_pair(linvr[2 * t], linvr[2 * t + 1])
        both.append(factor)
        turned = dot_nn(factor, srr[2 * t : 2 * t + 2].reshape(128, 128).astype(F32), HIGHEST).T
        rows[...] = turned.reshape(8, 16, 128)
        value = rows[z]
        basis_ref[res_of(t, 0)] = value[:, 0:64]
        basis_ref[res_of(t, 1)] = pltpu.roll(value, 64, 1)[:, 0:64]
    for copy in got_a + got_b:
        copy.wait_recv()
    first, second = fa[z], fb[y]
    for d in range(7):
        first = first + ria2[d]
        second = second + rib2[d]
    for t in range(NX):
        half = first if t < 2 else second
        value = dot_nt(half[:, 128 * (t % 2) : 128 * (t % 2) + 128], both[t], HIGHEST)
        image_ref[res_of(t, 0)] = value[:, 0:64]
        image_ref[res_of(t, 1)] = pltpu.roll(value, 64, 1)[:, 0:64]
    for copy in pending:
        copy.wait_send()


def local(
    left_u,
    left_v,
    left_rank,
    right_u,
    right_v,
    right_rank,
    near_tiles,
    near_block,
    comp_rank,
    omega,
):
    vmem = pl.BlockSpec(memory_space=pltpu.VMEM)
    smem = pl.BlockSpec(memory_space=pltpu.SMEM)
    scratch = [
        ((4, 64, 1024), BF),
        ((4, 64, 1024), BF),
        ((4, 64, 1024), BF),
        ((4, 64, 1024), BF),
        ((1024, 1024), BF),
        ((64, 1024), BF),
        ((4, 4, 128, 1024), BF),
        ((4, 128, 1024), BF),
        ((256, 1024), BF),
        ((4, 64, 1024), BF),
        ((256, 1024), BF),
        ((8, 64, 256), BF),
        ((8, 64, 256), BF),
        ((8, 32, 1024), BF),
        ((8, 8, 32, 128), BF),
        ((7, 32, 1024), BF),
        ((7, 8, 32, 128), BF),
        ((8, 32, 128), F32),
        ((8, 32, 128), F32),
        ((7, 32, 128), F32),
        ((7, 32, 128), F32),
        ((8, 64, 1024), BF),
        ((32, 128), F32),
        ((7, 32, 128), F32),
        ((8, 32, 128), F32),
        ((8, 32, 128), F32),
        ((8, 64, 128), BF),
        ((8, 64, 256), BF),
        ((8, 64, 256), BF),
        ((512, 1024), BF),
        ((4, 512, 64), BF),
        ((8, 256, 1024), BF),
        ((8, 8, 128), F32),
        ((8, 8, 128), F32),
        ((8, 256, 128), BF),
        ((8, 8, 16, 256), BF),
        ((7, 256, 128), BF),
        ((7, 8, 16, 256), BF),
        ((8, 16, 256), F32),
        ((8, 16, 256), F32),
        ((7, 16, 256), F32),
        ((7, 16, 256), F32),
        ((8, 16, 128), F32),
    ]
    basis, image = pl.pallas_call(
        kernel,
        out_shape=[jax.ShapeDtypeStruct((8, 16, 64), F32)] * 2,
        in_specs=[pl.BlockSpec(memory_space=pl.ANY)] * 6 + [smem] * 4,
        out_specs=[vmem, vmem],
        scratch_shapes=[pltpu.VMEM(shape, dtype) for shape, dtype in scratch]
        + [pltpu.SemaphoreType.DMA((6,)), pltpu.SemaphoreType.DMA((COPIES,)), pltpu.SemaphoreType.DMA((COPIES,))],
        compiler_params=pltpu.CompilerParams(
            collective_id=0, has_side_effects=True, vmem_limit_bytes=60 * 1024 * 1024
        ),
    )(
        jnp.swapaxes(left_v[0], 1, 2),
        jnp.swapaxes(left_u[0], 1, 2),
        jnp.swapaxes(right_u[:, 0], 1, 2),
        jnp.swapaxes(right_v[:, 0], 1, 2),
        near_tiles[0, 0],
        jnp.swapaxes(omega[0], 0, 1),
        left_rank,
        right_rank.T,
        near_block,
        comp_rank.T,
    )
    return basis[:, None], image[:, None]


def solution(mesh):
    placed = (
        P("res", "inner", None, None),
        P("res", "inner", None, None),
        P("res", "inner"),
        P("inner", "res", None, None),
        P("inner", "res", None, None),
        P("inner", "res"),
        P("inner", "res", None, None),
        P("inner", "res"),
        P(None, "res"),
        P("res", None, None),
    )
    return jax.shard_map(
        local,
        mesh=mesh,
        in_specs=placed,
        out_specs=(P(None, "res", "inner", None), P(None, "res", "inner", None)),
        check_vma=False,
    )
```

```python
import jax
import jax.numpy as jnp
from jax import lax
from jax.experimental import pallas as pl
from jax.experimental.pallas import tpu as pltpu
from jax.sharding import PartitionSpec as P

BF = jnp.bfloat16
F32 = jnp.float32
MESH = pl.DeviceIdType.MESH
HIGHEST = lax.Precision.HIGHEST
NY = 8
NZ = 8
NX = 4
COPIES = 180


def dot_nn(a, b, precision=None):
    return lax.dot_general(a, b, (((1,), (0,)), ((), ())), precision=precision, preferred_element_type=F32)


def dot_nt(a, b, precision=None):
    return lax.dot_general(a, b, (((1,), (1,)), ((), ())), precision=precision, preferred_element_type=F32)


def lanes(shape):
    return lax.broadcasted_iota(jnp.int32, shape, len(shape) - 1)


def row_mask(rank, shape):
    rows = lax.broadcasted_iota(jnp.int32, shape, 0)
    return jnp.where(rows < rank, 1.0, 0.0).astype(BF)


def unpack_with_identity(gram):
    lane32 = lanes((32, 128))
    rows32 = lax.broadcasted_iota(jnp.int32, (32, 128), 0)
    top = jnp.where(lane32 < 64, gram, jnp.where(lane32 - 64 == rows32, 1.0, 0.0))
    bottom = jnp.where(lane32 < 64, pltpu.roll(gram, 64, 1), jnp.where(lane32 - 96 == rows32, 1.0, 0.0))
    return [top[8 * b : 8 * b + 8] for b in range(4)] + [bottom[8 * b : 8 * b + 8] for b in range(4)]


def eliminate(blocks, first, last):
    rows8 = lax.broadcasted_iota(jnp.int32, (8, 128), 0)
    for k in range(first, last):
        kb, kr = k // 8, k % 8
        row = blocks[kb][kr : kr + 1, :]
        scaled = row / row[:, k : k + 1]
        for b in range(kb, 8):
            update = blocks[b][:, k : k + 1] * scaled
            if b == kb:
                update = jnp.where(rows8 > kr, update, 0.0)
            blocks[b] = blocks[b] - update


def inverse_of(blocks):
    lane8 = lanes((8, 128))
    lane32 = lanes((32, 128))
    rows8 = lax.broadcasted_iota(jnp.int32, (8, 128), 0)
    scaled = []
    for b in range(8):
        diagonal = jnp.sum(jnp.where(lane8 == rows8 + 8 * b, blocks[b], 0.0), axis=1, keepdims=True)
        scaled.append(blocks[b] * (1.0 / jnp.sqrt(diagonal)))
    top = jnp.concatenate(scaled[:4], axis=0)
    bottom = jnp.concatenate(scaled[4:], axis=0)
    return jnp.where(lane32 < 64, pltpu.roll(top, 64, 1), bottom)


def block_pair(first, second):
    lane32 = lanes((32, 128))
    left = lane32 < 64
    return jnp.concatenate(
        [
            jnp.where(left, first, 0.0),
            jnp.where(left, pltpu.roll(first, 64, 1), 0.0),
            jnp.where(left, 0.0, pltpu.roll(second, 64, 1)),
            jnp.where(left, 0.0, second),
        ],
        axis=0,
    )


def kernel(
    lv_hbm,
    lu_hbm,
    ru_hbm,
    rv_hbm,
    near_hbm,
    omega_hbm,
    left_rank,
    right_rank,
    near_block,
    comp_rank,
    basis_ref,
    image_ref,
    lv_ref,
    lu_ref,
    ru_ref,
    rv_ref,
    near_ref,
    omega_ref,
    lvb,
    wt,
    lum,
    rum,
    rvm,
    exs,
    exr,
    ska,
    skb,
    ra,
    rb,
    sa,
    sb,
    ra2,
    rb2,
    sfull,
    gs,
    gr,
    linvg,
    linvr,
    srr,
    ut,
    utr,
    lvsel,
    held,
    wgt,
    act,
    actr,
    ia,
    ib,
    ria,
    rib,
    fa,
    fb,
    ria2,
    rib2,
    rows,
    load_sem,
    send_sem,
    recv_sem,
):
    p = lax.axis_index("inner")
    r = lax.axis_index("res")
    y, z = p // NZ, p % NZ
    x, c = r // 2, r % 2
    used = [0]
    moves = (
        (lv_hbm, lv_ref),
        (rv_hbm, rv_ref),
        (omega_hbm, omega_ref),
        (ru_hbm, ru_ref),
        (near_hbm, near_ref),
        (lu_hbm, lu_ref),
    )
    loads = [pltpu.make_async_copy(src, dst, load_sem.at[n]) for n, (src, dst) in enumerate(moves)]
    for load in loads:
        load.start()

    def at_y(d):
        return (lax.rem(y + d, NY) * NZ + z, r)

    def at_z(d):
        return (y * NZ + lax.rem(z + d, NZ), r)

    def at_res(q, par):
        return (p, lax.rem(x + q, NX) * 2 + (c if par == 0 else 1 - c))

    def res_of(q, par):
        return lax.rem(x + q, NX) * 2 + (c if par == 0 else 1 - c)

    def start(src, dst, device):
        n = used[0]
        used[0] += 1
        copy = pltpu.make_async_remote_copy(
            src_ref=src,
            dst_ref=dst,
            send_sem=send_sem.at[n],
            recv_sem=recv_sem.at[n],
            device_id=device,
            device_id_type=MESH,
        )
        copy.start()
        pending.append(copy)
        return copy

    pending = []

    def start_unless_own(distance, src, lands, base, device):
        n = lax.rem(distance + 7, 8)

        @pl.when(distance != 0)
        def _():
            pltpu.make_async_remote_copy(
                src_ref=src,
                dst_ref=lands.at[n],
                send_sem=send_sem.at[base + n],
                recv_sem=recv_sem.at[base + n],
                device_id=device,
                device_id_type=MESH,
            ).start()

    pairs = [(q, par) for q in range(NX) for par in range(2)]
    others = pairs[1:]
    back = {(q, par): ((NX - q) % NX) * 2 + par for q, par in pairs}

    barrier = pltpu.get_barrier_semaphore()
    for d in range(1, NY):
        pl.semaphore_signal(barrier, inc=1, device_id=at_y(d), device_id_type=MESH)
    for d in range(1, NZ):
        pl.semaphore_signal(barrier, inc=1, device_id=at_z(d), device_id_type=MESH)
    for q, par in others:
        pl.semaphore_signal(barrier, inc=1, device_id=at_res(q, par), device_id_type=MESH)

    loads[0].wait()
    for k in range(4):
        lvb[k, 0, 0:64, :] = lv_ref[k] * row_mask(left_rank[0, k], (64, 1024))
    pl.semaphore_wait(barrier, NY - 1 + NZ - 1 + 7)

    nb = near_block[0, 0]

    def pick_near(q):
        rows = slice(128 * q, 128 * q + 128)
        kept = jnp.zeros((128, 1024), BF)
        for k in range(4):
            kept = jnp.where(nb == k, lvb[k, q], kept)
            held[k, rows, :] = dot_nt(lvb[k, q], rum[k]).astype(BF)
        lvsel[rows, :] = kept

    def make_weights(n):
        cols = slice(256 * n, 256 * n + 256)
        tile = near_ref[:, cols]
        for q in range(NX):
            rows = slice(128 * q, 128 * q + 128)
            near_part = dot_nn(lvsel[rows, :], tile)
            for k in range(4):
                far_part = dot_nn(held[k, rows, :], rvm[64 * k : 64 * k + 64, cols])
                value = jnp.where(nb == k, near_part, far_part).astype(BF)
                wgt[2 * q, 64 * k : 64 * k + 64, cols] = value[0:64]
                wgt[2 * q + 1, 64 * k : 64 * k + 64, cols] = value[64:128]

    def piece_of(step, n):
        return lambda: step(n)

    weight_work = [piece_of(pick_near, q) for q in range(4)] + [piece_of(make_weights, n) for n in range(4)]

    sibling = at_res(0, 1)
    sib_own = start(lvb.at[:, 0, 0:64], lvb.at[:, 0, 64:128], sibling)
    came_v = {}
    for k in range(4):
        turned = (k + 2) % 4
        came_v[3, k] = start(lvb.at[k, 0, 0:64], lvb.at[k, 3, 0:64], at_res(1, 0))
        came_v[1, turned] = start(lvb.at[turned, 0, 0:64], lvb.at[turned, 1, 0:64], at_res(3, 0))

    act_came = []
    for q, par in pairs:
        lane8 = lanes((8, 128)) % 64
        unused = jnp.where(lane8 < comp_rank[0, res_of(q, par)], 0.0, 1.0)
        if (q, par) == (0, 0):
            actr[0] = unused
        else:
            act[2 * q + par] = unused
            act_came.append(start(act.at[2 * q + par], actr.at[back[(q, par)]], at_res(q, par)))

    for load in loads[1:]:
        load.wait()
    for k in range(4):
        mask = row_mask(right_rank[0, k], (64, 1024))
        rum[k] = ru_ref[k] * mask
        rvm[64 * k : 64 * k + 64, :] = rv_ref[k] * mask
        lum[64 * k : 64 * k + 64, :] = lu_ref[k] * row_mask(left_rank[0, k], (64, 1024))
    omega = omega_ref[...]
    mixed = [dot_nt(omega, rvm[64 * k : 64 * k + 64, :]) for k in range(4)]
    for n in range(4):
        cols = slice(256 * n, 256 * n + 256)
        near_omega = dot_nt(omega, near_ref[cols, :])
        for k in range(4):
            high = mixed[k].astype(BF)
            low = (mixed[k] - high.astype(F32)).astype(BF)
            part = dot_nn(high, rum[k, :, cols]) + dot_nn(low, rum[k, :, cols])
            full = jnp.where(nb == k, near_omega, part)
            high = full.astype(BF)
            wt[k, 0:64, cols] = high
            wt[k, 64:128, cols] = (full - high.astype(F32)).astype(BF)

    def expand_chip(q):
        lane = lanes((64, 128))
        parts = []
        for k in range(4):
            both = dot_nt(wt[k], lvb[k, q])
            parts.append(both[0:64] + both[64:128])
        rolled = [pltpu.roll(part, 64, 1) for part in parts]
        for par in range(2):
            if par == 0:
                tiles = [jnp.where(lane < 64, parts[2 * t], rolled[2 * t + 1]) for t in range(2)]
            else:
                tiles = [jnp.where(lane < 64, rolled[2 * t], parts[2 * t + 1]) for t in range(2)]
            active = row_mask(comp_rank[0, res_of(q, par)], (64, 128))
            for t in range(2):
                value = tiles[t].astype(BF) * active
                if (q, par) == (0, 0):
                    exr[0, :, 128 * t : 128 * t + 128] = value
                else:
                    exs[2 * q + par, :, 128 * t : 128 * t + 128] = value

    came = {}

    def send_expand(q, par):
        slot = back[(q, par)]
        came[slot] = start(exs.at[2 * q + par], exr.at[slot], at_res(q, par))

    sib_own.wait_recv()
    expand_chip(0)
    send_expand(0, 1)

    fwd = {1: [], 2: [], 3: []}

    def forward(q, k):
        came_v[q, k].wait_recv()
        if (q, k) in ((3, 0), (3, 1)):
            came_v[2, k] = start(lvb.at[k, 3, 0:64], lvb.at[k, 2, 0:64], at_res(1, 0))
        if (q, k) in ((1, 2), (1, 3)):
            came_v[2, k] = start(lvb.at[k, 1, 0:64], lvb.at[k, 2, 0:64], at_res(3, 0))
        fwd[q].append(start(lvb.at[k, q, 0:64], lvb.at[k, q, 64:128], sibling))

    def expand_and_send(q):
        for copy in fwd[q]:
            copy.wait_recv()
        expand_chip(q)
        send_expand(q, 0)
        send_expand(q, 1)

    def slot_of(column):
        return lax.rem(column // 2 - x + NX, NX) * 2 + lax.rem(column + c, 2)

    place = {0: 0, 3: 1, 1: 2, 2: 3}

    def sketch_chip(q):
        for par in range(2):
            if (q, par) != (0, 0):
                came[2 * q + par].wait_recv()
        factor = exr[2 * q : 2 * q + 2].reshape(128, 256)
        for n in range(4):
            part = dot_nn(factor, lum[:, 256 * n : 256 * n + 256]).astype(BF)
            for par in range(2):
                ska[2 * q + par, :, 256 * n : 256 * n + 256] = part[64 * par : 64 * par + 32]
                for t in range(2):
                    tile = part[64 * par + 32 : 64 * par + 64, 128 * t : 128 * t + 128]
                    skb[2 * n + t, 2 * place[q] + par] = tile
        for par in range(2):
            column = res_of(q, par)
            distance = lax.rem(column - y + NY, NY)
            start_unless_own(distance, ska.at[2 * q + par], ra, sums_base, (column * NZ + z, r))

    got_b = []

    def send_high(tiles):
        for d in range(1, NZ):
            got_b.append(start(skb.at[lax.rem(z + d, NZ), tiles], rb.at[d - 1, tiles], at_z(d)))

    sums_base = used[0]
    used[0] += 7
    got_a = []
    for d in range(7):
        got_a.append(
            pltpu.make_async_remote_copy(
                src_ref=ska.at[0],
                dst_ref=ra.at[d],
                send_sem=send_sem.at[sums_base + d],
                recv_sem=recv_sem.at[sums_base + d],
                device_id=at_y(d + 1),
                device_id_type=MESH,
            )
        )
    pending.extend(got_a)
    for k in range(4):
        forward(3, k)
        forward(1, (k + 2) % 4)
    expand_and_send(3)
    expand_and_send(1)
    sketch_chip(0)
    for k in (0, 2, 1, 3):
        forward(2, k)
    expand_and_send(2)
    sketch_chip(3)
    sketch_chip(1)
    send_high(slice(0, 6))
    sketch_chip(2)
    send_high(slice(6, 8))
    for piece in weight_work:
        piece()
    for copy in got_a:
        copy.wait_recv()
    mine = slot_of(y)
    for n in range(8):
        cols = slice(128 * n, 128 * n + 128)
        total = ska[mine, :, cols].astype(F32)
        for d in range(7):
            total = total + ra[d, :, cols].astype(F32)
        sa[n] = total
    got_a = [start(sa.at[lax.rem(z + d, NZ)], ra2.at[d - 1], at_z(d)) for d in range(1, 8)]
    for copy in got_b:
        copy.wait_recv()
    for q, par in pairs:
        n = 2 * place[q] + par
        total = skb[z, n].astype(F32)
        for d in range(7):
            total = total + rb[d, n].astype(F32)
        sb[2 * q + par] = total
    got_b = [start(sb.at[slot_of(lax.rem(y + d, NY))], rb2.at[d - 1], at_y(d)) for d in range(1, 8)]
    for copy in got_a + got_b:
        copy.wait_recv()
    low_half = sa[z]
    high_half = sb[mine]
    for d in range(7):
        low_half = low_half + ra2[d]
        high_half = high_half + rb2[d]

    zcols = pl.ds(pl.multiple_of(z * 128, 128), 128)
    sfull[y, 0:32, zcols] = low_half.astype(BF)
    sfull[y, 32:64, zcols] = high_half.astype(BF)
    got_a, got_b = [], []
    for d in range(1, 8):
        got_a.append(start(sfull.at[y, 0:32, zcols], sfull.at[y, 0:32, zcols], at_z(d)))
        got_b.append(start(sfull.at[y, 32:64, zcols], sfull.at[y, 32:64, zcols], at_y(d)))

    part = jnp.concatenate([low_half, high_half], axis=0)
    twice = jnp.concatenate([part, part], axis=0)
    gram = dot_nt(part, twice, HIGHEST)
    gs[...] = jnp.where(lanes((32, 128)) < 64, gram[0:32], gram[32:64])
    got_gram = [start(gs, gr.at[d - 1], at_z(d)) for d in range(1, 8)]

    for copy in got_a:
        copy.wait_recv()
    spread = [start(sfull.at[y, 0:32], sfull.at[y, 0:32], at_y(d)) for d in range(1, 8)]
    for copy in got_b:
        copy.wait_recv()
    spread += [start(sfull.at[:, 32:64, zcols], sfull.at[:, 32:64, zcols], at_z(d)) for d in range(1, 8)]

    blocks = []

    def sum_gram():
        for copy in got_gram + act_came:
            copy.wait_recv()
        total = gs[...]
        for d in range(7):
            total = total + gr[d]
        lane32 = lanes((32, 128))
        rows32 = lax.broadcasted_iota(jnp.int32, (32, 128), 0)
        index = jnp.where(lane32 < 64, rows32, rows32 + 32)
        unused = jnp.where(lane32 % 64 == index, actr[mine, 0:1, :], 0.0)
        blocks.extend(unpack_with_identity(total + unused))

    sum_gram()
    eliminate(blocks, 0, 40)
    for copy in spread:
        copy.wait_recv()

    for j in range(0, 8, 2):
        value = dot_nt(sfull[j : j + 2].reshape(128, 1024), lum[...]).astype(BF)
        ut[j] = value[0:64]
        ut[j + 1] = value[64:128]
    came = {}
    for q, par in others:
        came[back[(q, par)]] = start(ut.at[res_of(q, par)], utr.at[back[(q, par)]], at_res(q, par))
    utr[0] = ut[r]
    row_cols = pl.ds(pl.multiple_of(y * 128, 128), 128)
    rows_came = []
    for q, par in others:
        rows_came.append(start(sfull.at[res_of(q, par), :, row_cols], srr.at[back[(q, par)]], at_res(q, par)))
    srr[0] = sfull[r, :, row_cols]
    eliminate(blocks, 40, 64)
    linvg[y] = inverse_of(blocks)
    got_inverse = [start(linvg.at[y], linvg.at[y], at_y(d)) for d in range(1, 8)]

    for slot in range(4):
        if slot:
            came[slot].wait_recv()
        for n in range(4):
            part = dot_nn(utr[slot], wgt[slot, :, 256 * n : 256 * n + 256])
            for t in range(2):
                tile = part[:, 128 * t : 128 * t + 128]
                ia[2 * n + t, 64 * slot : 64 * slot + 64, :] = tile.astype(BF)
    got_a = [start(ia.at[lax.rem(y + d, NY)], ria.at[d - 1], at_y(d)) for d in range(1, 8)]
    for pair in (1, 0):
        slot = 4 + 2 * pair
        came[slot].wait_recv()
        came[slot + 1].wait_recv()
        for n in range(4):
            cols = slice(256 * n, 256 * n + 256)
            part = jnp.concatenate(
                [dot_nn(utr[slot], wgt[slot, :, cols]), dot_nn(utr[slot + 1], wgt[slot + 1, :, cols])], axis=0
            )
            for t in range(2):
                turned = part[:, 128 * t : 128 * t + 128].T.astype(BF)
                ib[:, 2 * n + t, :, 128 * pair : 128 * pair + 128] = turned.reshape(8, 16, 128)
    got_b = [start(ib.at[lax.rem(z + d, NZ)], rib.at[d - 1], at_z(d)) for d in range(1, 8)]
    for copy in got_inverse:
        copy.wait_recv()
    inverse_came = []
    for q, par in others:
        inverse_came.append(start(linvg.at[res_of(q, par)], linvr.at[back[(q, par)]], at_res(q, par)))
    linvr[0] = linvg[r]
    for copy in got_a:
        copy.wait_recv()
    total = ia[y].astype(F32)
    for d in range(7):
        total = total + ria[d].astype(F32)
    fa[...] = total.T.reshape(8, 16, 256)
    got_a = [start(fa.at[lax.rem(z + d, NZ)], ria2.at[d - 1], at_z(d)) for d in range(1, 8)]
    for copy in got_b:
        copy.wait_recv()
    for n in range(8):
        total = ib[z, n].astype(F32)
        for d in range(7):
            total = total + rib[d, n].astype(F32)
        fb[n] = total
    got_b = [start(fb.at[lax.rem(y + d, NY)], rib2.at[d - 1], at_y(d)) for d in range(1, 8)]

    for copy in rows_came + inverse_came:
        copy.wait_recv()
    both = []
    for t in range(NX):
        factor = block_pair(linvr[2 * t], linvr[2 * t + 1])
        both.append(factor)
        turned = dot_nn(factor, srr[2 * t : 2 * t + 2].reshape(128, 128).astype(F32), HIGHEST).T
        rows[...] = turned.reshape(8, 16, 128)
        value = rows[z]
        basis_ref[res_of(t, 0)] = value[:, 0:64]
        basis_ref[res_of(t, 1)] = pltpu.roll(value, 64, 1)[:, 0:64]
    for copy in got_a + got_b:
        copy.wait_recv()
    first, second = fa[z], fb[y]
    for d in range(7):
        first = first + ria2[d]
        second = second + rib2[d]
    for t in range(NX):
        half = first if t < 2 else second
        value = dot_nt(half[:, 128 * (t % 2) : 128 * (t % 2) + 128], both[t], HIGHEST)
        image_ref[res_of(t, 0)] = value[:, 0:64]
        image_ref[res_of(t, 1)] = pltpu.roll(value, 64, 1)[:, 0:64]
    for copy in pending:
        copy.wait_send()


def local(
    left_u,
    left_v,
    left_rank,
    right_u,
    right_v,
    right_rank,
    near_tiles,
    near_block,
    comp_rank,
    omega,
):
    vmem = pl.BlockSpec(memory_space=pltpu.VMEM)
    smem = pl.BlockSpec(memory_space=pltpu.SMEM)
    scratch = [
        ((4, 64, 1024), BF),
        ((4, 64, 1024), BF),
        ((4, 64, 1024), BF),
        ((4, 64, 1024), BF),
        ((1024, 1024), BF),
        ((64, 1024), BF),
        ((4, 4, 128, 1024), BF),
        ((4, 128, 1024), BF),
        ((256, 1024), BF),
        ((4, 64, 1024), BF),
        ((256, 1024), BF),
        ((8, 64, 256), BF),
        ((8, 64, 256), BF),
        ((8, 32, 1024), BF),
        ((8, 8, 32, 128), BF),
        ((7, 32, 1024), BF),
        ((7, 8, 32, 128), BF),
        ((8, 32, 128), F32),
        ((8, 32, 128), F32),
        ((7, 32, 128), F32),
        ((7, 32, 128), F32),
        ((8, 64, 1024), BF),
        ((32, 128), F32),
        ((7, 32, 128), F32),
        ((8, 32, 128), F32),
        ((8, 32, 128), F32),
        ((8, 64, 128), BF),
        ((8, 64, 256), BF),
        ((8, 64, 256), BF),
        ((512, 1024), BF),
        ((4, 512, 64), BF),
        ((8, 256, 1024), BF),
        ((8, 8, 128), F32),
        ((8, 8, 128), F32),
        ((8, 256, 128), BF),
        ((8, 8, 16, 256), BF),
        ((7, 256, 128), BF),
        ((7, 8, 16, 256), BF),
        ((8, 16, 256), F32),
        ((8, 16, 256), F32),
        ((7, 16, 256), F32),
        ((7, 16, 256), F32),
        ((8, 16, 128), F32),
    ]
    basis, image = pl.pallas_call(
        kernel,
        out_shape=[jax.ShapeDtypeStruct((8, 16, 64), F32)] * 2,
        in_specs=[pl.BlockSpec(memory_space=pl.ANY)] * 6 + [smem] * 4,
        out_specs=[vmem, vmem],
        scratch_shapes=[pltpu.VMEM(shape, dtype) for shape, dtype in scratch]
        + [pltpu.SemaphoreType.DMA((6,)), pltpu.SemaphoreType.DMA((COPIES,)), pltpu.SemaphoreType.DMA((COPIES,))],
        compiler_params=pltpu.CompilerParams(
            collective_id=0, has_side_effects=True, vmem_limit_bytes=60 * 1024 * 1024
        ),
    )(
        jnp.swapaxes(left_v[0], 1, 2),
        jnp.swapaxes(left_u[0], 1, 2),
        jnp.swapaxes(right_u[:, 0], 1, 2),
        jnp.swapaxes(right_v[:, 0], 1, 2),
        near_tiles[0, 0],
        jnp.swapaxes(omega[0], 0, 1),
        left_rank,
        right_rank.T,
        near_block,
        comp_rank.T,
    )
    return basis[:, None], image[:, None]


def solution(mesh):
    placed = (
        P("res", "inner", None, None),
        P("res", "inner", None, None),
        P("res", "inner"),
        P("inner", "res", None, None),
        P("inner", "res", None, None),
        P("inner", "res"),
        P("inner", "res", None, None),
        P("inner", "res"),
        P(None, "res"),
        P("res", None, None),
    )
    return jax.shard_map(
        local,
        mesh=mesh,
        in_specs=placed,
        out_specs=(P(None, "res", "inner", None), P(None, "res", "inner", None)),
        check_vma=False,
    )
```

```python
import jax
import jax.numpy as jnp
from jax import lax
from jax.experimental import pallas as pl
from jax.experimental.pallas import tpu as pltpu
from jax.sharding import PartitionSpec as P

BF = jnp.bfloat16
F32 = jnp.float32
MESH = pl.DeviceIdType.MESH
HIGHEST = lax.Precision.HIGHEST
NY = 8
NZ = 8
NX = 4
FAR_FIRST = (4, 3, 5, 2, 6, 1, 7)
COPIES = 180


def dot_nn(a, b, precision=None):
    return lax.dot_general(a, b, (((1,), (0,)), ((), ())), precision=precision, preferred_element_type=F32)


def dot_nt(a, b, precision=None):
    return lax.dot_general(a, b, (((1,), (1,)), ((), ())), precision=precision, preferred_element_type=F32)


def lanes(shape):
    return lax.broadcasted_iota(jnp.int32, shape, len(shape) - 1)


def row_mask(rank, shape):
    rows = lax.broadcasted_iota(jnp.int32, shape, 0)
    return jnp.where(rows < rank, 1.0, 0.0).astype(BF)


def unpack_with_identity(gram):
    lane32 = lanes((32, 128))
    rows32 = lax.broadcasted_iota(jnp.int32, (32, 128), 0)
    top = jnp.where(lane32 < 64, gram, jnp.where(lane32 - 64 == rows32, 1.0, 0.0))
    bottom = jnp.where(lane32 < 64, pltpu.roll(gram, 64, 1), jnp.where(lane32 - 96 == rows32, 1.0, 0.0))
    return [top[8 * b : 8 * b + 8] for b in range(4)] + [bottom[8 * b : 8 * b + 8] for b in range(4)]


def eliminate(blocks, first, last):
    rows8 = lax.broadcasted_iota(jnp.int32, (8, 128), 0)
    for k in range(first, last):
        kb, kr = k // 8, k % 8
        row = blocks[kb][kr : kr + 1, :]
        scaled = row / row[:, k : k + 1]
        for b in range(kb, 8):
            update = blocks[b][:, k : k + 1] * scaled
            if b == kb:
                update = jnp.where(rows8 > kr, update, 0.0)
            blocks[b] = blocks[b] - update


def inverse_of(blocks):
    lane8 = lanes((8, 128))
    lane32 = lanes((32, 128))
    rows8 = lax.broadcasted_iota(jnp.int32, (8, 128), 0)
    scaled = []
    for b in range(8):
        diagonal = jnp.sum(jnp.where(lane8 == rows8 + 8 * b, blocks[b], 0.0), axis=1, keepdims=True)
        scaled.append(blocks[b] * (1.0 / jnp.sqrt(diagonal)))
    top = jnp.concatenate(scaled[:4], axis=0)
    bottom = jnp.concatenate(scaled[4:], axis=0)
    return jnp.where(lane32 < 64, pltpu.roll(top, 64, 1), bottom)


def block_pair(first, second):
    lane32 = lanes((32, 128))
    left = lane32 < 64
    return jnp.concatenate(
        [
            jnp.where(left, first, 0.0),
            jnp.where(left, pltpu.roll(first, 64, 1), 0.0),
            jnp.where(left, 0.0, pltpu.roll(second, 64, 1)),
            jnp.where(left, 0.0, second),
        ],
        axis=0,
    )


def kernel(
    lv_hbm,
    lu_hbm,
    ru_hbm,
    rv_hbm,
    near_hbm,
    omega_hbm,
    left_rank,
    right_rank,
    near_block,
    comp_rank,
    basis_ref,
    image_ref,
    lv_ref,
    lu_ref,
    ru_ref,
    rv_ref,
    near_ref,
    omega_ref,
    lvb,
    wt,
    lum,
    rum,
    rvm,
    exs,
    exr,
    ska,
    skb,
    ra,
    rb,
    sa,
    sb,
    ra2,
    rb2,
    sfull,
    gs,
    gr,
    linvg,
    linvr,
    srr,
    ut,
    utr,
    lvsel,
    held,
    wgt,
    act,
    actr,
    ia,
    ib,
    ria,
    rib,
    fa,
    fb,
    ria2,
    rib2,
    rows,
    load_sem,
    send_sem,
    recv_sem,
):
    p = lax.axis_index("inner")
    r = lax.axis_index("res")
    y, z = p // NZ, p % NZ
    x, c = r // 2, r % 2
    used = [0]
    moves = (
        (lv_hbm, lv_ref),
        (rv_hbm, rv_ref),
        (omega_hbm, omega_ref),
        (ru_hbm, ru_ref),
        (near_hbm, near_ref),
        (lu_hbm, lu_ref),
    )
    loads = [pltpu.make_async_copy(src, dst, load_sem.at[n]) for n, (src, dst) in enumerate(moves)]
    for load in loads:
        load.start()

    def at_y(d):
        return (lax.rem(y + d, NY) * NZ + z, r)

    def at_z(d):
        return (y * NZ + lax.rem(z + d, NZ), r)

    def at_res(q, par):
        return (p, lax.rem(x + q, NX) * 2 + (c if par == 0 else 1 - c))

    def res_of(q, par):
        return lax.rem(x + q, NX) * 2 + (c if par == 0 else 1 - c)

    def start(src, dst, device):
        n = used[0]
        used[0] += 1
        copy = pltpu.make_async_remote_copy(
            src_ref=src,
            dst_ref=dst,
            send_sem=send_sem.at[n],
            recv_sem=recv_sem.at[n],
            device_id=device,
            device_id_type=MESH,
        )
        copy.start()
        pending.append(copy)
        return copy

    pending = []

    def start_unless_own(distance, src, lands, base, device):
        n = lax.rem(distance + 7, 8)

        @pl.when(distance != 0)
        def _():
            pltpu.make_async_remote_copy(
                src_ref=src,
                dst_ref=lands.at[n],
                send_sem=send_sem.at[base + n],
                recv_sem=recv_sem.at[base + n],
                device_id=device,
                device_id_type=MESH,
            ).start()

    pairs = [(q, par) for q in range(NX) for par in range(2)]
    others = pairs[1:]
    back = {(q, par): ((NX - q) % NX) * 2 + par for q, par in pairs}

    barrier = pltpu.get_barrier_semaphore()
    for d in range(1, NY):
        pl.semaphore_signal(barrier, inc=1, device_id=at_y(d), device_id_type=MESH)
    for d in range(1, NZ):
        pl.semaphore_signal(barrier, inc=1, device_id=at_z(d), device_id_type=MESH)
    for q, par in others:
        pl.semaphore_signal(barrier, inc=1, device_id=at_res(q, par), device_id_type=MESH)

    loads[0].wait()
    for k in range(4):
        lvb[k, 0, 0:64, :] = lv_ref[k] * row_mask(left_rank[0, k], (64, 1024))
    pl.semaphore_wait(barrier, NY - 1 + NZ - 1 + 7)

    nb = near_block[0, 0]

    def pick_near(q):
        rows = slice(128 * q, 128 * q + 128)
        kept = jnp.zeros((128, 1024), BF)
        for k in range(4):
            kept = jnp.where(nb == k, lvb[k, q], kept)
            held[k, rows, :] = dot_nt(lvb[k, q], rum[k]).astype(BF)
        lvsel[rows, :] = kept

    def make_weights(n):
        cols = slice(256 * n, 256 * n + 256)
        tile = near_ref[:, cols]
        for q in range(NX):
            rows = slice(128 * q, 128 * q + 128)
            near_part = dot_nn(lvsel[rows, :], tile)
            for k in range(4):
                far_part = dot_nn(held[k, rows, :], rvm[64 * k : 64 * k + 64, cols])
                value = jnp.where(nb == k, near_part, far_part).astype(BF)
                wgt[2 * q, 64 * k : 64 * k + 64, cols] = value[0:64]
                wgt[2 * q + 1, 64 * k : 64 * k + 64, cols] = value[64:128]

    def piece_of(step, n):
        return lambda: step(n)

    weight_work = [piece_of(pick_near, q) for q in range(4)] + [piece_of(make_weights, n) for n in range(4)]

    sibling = at_res(0, 1)
    sib_own = start(lvb.at[:, 0, 0:64], lvb.at[:, 0, 64:128], sibling)
    came_v = {}
    for k in range(4):
        turned = (k + 2) % 4
        came_v[3, k] = start(lvb.at[k, 0, 0:64], lvb.at[k, 3, 0:64], at_res(1, 0))
        came_v[1, turned] = start(lvb.at[turned, 0, 0:64], lvb.at[turned, 1, 0:64], at_res(3, 0))

    fwd = {1: [], 2: [], 3: []}

    def forward(q, k):
        came_v[q, k].wait_recv()
        if (q, k) in ((3, 0), (3, 1)):
            came_v[2, k] = start(lvb.at[k, 3, 0:64], lvb.at[k, 2, 0:64], at_res(1, 0))
        if (q, k) in ((1, 2), (1, 3)):
            came_v[2, k] = start(lvb.at[k, 1, 0:64], lvb.at[k, 2, 0:64], at_res(3, 0))
        fwd[q].append(start(lvb.at[k, q, 0:64], lvb.at[k, q, 64:128], sibling))

    act_came = []
    for q, par in pairs:
        lane8 = lanes((8, 128)) % 64
        unused = jnp.where(lane8 < comp_rank[0, res_of(q, par)], 0.0, 1.0)
        if (q, par) == (0, 0):
            actr[0] = unused
        else:
            act[2 * q + par] = unused
            act_came.append(start(act.at[2 * q + par], actr.at[back[(q, par)]], at_res(q, par)))

    for load in loads[1:]:
        load.wait()
    for k in range(4):
        mask = row_mask(right_rank[0, k], (64, 1024))
        rum[k] = ru_ref[k] * mask
        rvm[64 * k : 64 * k + 64, :] = rv_ref[k] * mask
        lum[64 * k : 64 * k + 64, :] = lu_ref[k] * row_mask(left_rank[0, k], (64, 1024))
    omega = omega_ref[...]
    mixed = [dot_nt(omega, rvm[64 * k : 64 * k + 64, :]) for k in range(4)]
    for n in range(4):
        cols = slice(256 * n, 256 * n + 256)
        near_omega = dot_nt(omega, near_ref[cols, :])
        for k in range(4):
            high = mixed[k].astype(BF)
            low = (mixed[k] - high.astype(F32)).astype(BF)
            part = dot_nn(high, rum[k, :, cols]) + dot_nn(low, rum[k, :, cols])
            full = jnp.where(nb == k, near_omega, part)
            high = full.astype(BF)
            wt[k, 0:64, cols] = high
            wt[k, 64:128, cols] = (full - high.astype(F32)).astype(BF)
        if n % 2:
            forward(3, n // 2)
            forward(1, n // 2 + 2)

    def expand_chip(q):
        lane = lanes((64, 128))
        parts = []
        for k in range(4):
            both = dot_nt(wt[k], lvb[k, q])
            parts.append(both[0:64] + both[64:128])
        rolled = [pltpu.roll(part, 64, 1) for part in parts]
        for par in range(2):
            if par == 0:
                tiles = [jnp.where(lane < 64, parts[2 * t], rolled[2 * t + 1]) for t in range(2)]
            else:
                tiles = [jnp.where(lane < 64, rolled[2 * t], parts[2 * t + 1]) for t in range(2)]
            active = row_mask(comp_rank[0, res_of(q, par)], (64, 128))
            for t in range(2):
                value = tiles[t].astype(BF) * active
                if (q, par) == (0, 0):
                    exr[0, :, 128 * t : 128 * t + 128] = value
                else:
                    exs[2 * q + par, :, 128 * t : 128 * t + 128] = value

    came = {}

    def send_expand(q, par):
        slot = back[(q, par)]
        came[slot] = start(exs.at[2 * q + par], exr.at[slot], at_res(q, par))

    sib_own.wait_recv()
    expand_chip(0)
    send_expand(0, 1)

    def expand_and_send(q):
        for copy in fwd[q]:
            copy.wait_recv()
        expand_chip(q)
        send_expand(q, 0)
        send_expand(q, 1)

    def slot_of(column):
        return lax.rem(column // 2 - x + NX, NX) * 2 + lax.rem(column + c, 2)

    place = {0: 0, 3: 1, 1: 2, 2: 3}

    def sketch_chip(q):
        for par in range(2):
            if (q, par) != (0, 0):
                came[2 * q + par].wait_recv()
        factor = exr[2 * q : 2 * q + 2].reshape(128, 256)
        for n in range(4):
            part = dot_nn(factor, lum[:, 256 * n : 256 * n + 256]).astype(BF)
            for par in range(2):
                ska[2 * q + par, :, 256 * n : 256 * n + 256] = part[64 * par : 64 * par + 32]
                for t in range(2):
                    tile = part[64 * par + 32 : 64 * par + 64, 128 * t : 128 * t + 128]
                    skb[2 * n + t, 2 * place[q] + par] = tile
        for par in range(2):
            column = res_of(q, par)
            distance = lax.rem(column - y + NY, NY)
            start_unless_own(distance, ska.at[2 * q + par], ra, sums_base, (column * NZ + z, r))

    got_b = []

    def send_high(tiles):
        for d in FAR_FIRST:
            got_b.append(start(skb.at[lax.rem(z + d, NZ), tiles], rb.at[d - 1, tiles], at_z(d)))

    sums_base = used[0]
    used[0] += 7
    got_a = []
    for d in range(7):
        got_a.append(
            pltpu.make_async_remote_copy(
                src_ref=ska.at[0],
                dst_ref=ra.at[d],
                send_sem=send_sem.at[sums_base + d],
                recv_sem=recv_sem.at[sums_base + d],
                device_id=at_y(d + 1),
                device_id_type=MESH,
            )
        )
    pending.extend(got_a)
    for k in (2, 3):
        forward(3, k)
        forward(1, k - 2)
    expand_and_send(3)
    expand_and_send(1)
    sketch_chip(0)
    for k in (0, 2, 1, 3):
        forward(2, k)
    expand_and_send(2)
    sketch_chip(3)
    sketch_chip(1)
    send_high(slice(0, 6))
    sketch_chip(2)
    send_high(slice(6, 8))
    for piece in weight_work:
        piece()
    for copy in got_a:
        copy.wait_recv()
    mine = slot_of(y)
    for n in range(8):
        cols = slice(128 * n, 128 * n + 128)
        total = ska[mine, :, cols].astype(F32)
        for d in range(7):
            total = total + ra[d, :, cols].astype(F32)
        sa[n] = total
    got_a = [start(sa.at[lax.rem(z + d, NZ)], ra2.at[d - 1], at_z(d)) for d in FAR_FIRST]
    for copy in got_b:
        copy.wait_recv()
    for q, par in pairs:
        n = 2 * place[q] + par
        total = skb[z, n].astype(F32)
        for d in range(7):
            total = total + rb[d, n].astype(F32)
        sb[2 * q + par] = total
    got_b = [start(sb.at[slot_of(lax.rem(y + d, NY))], rb2.at[d - 1], at_y(d)) for d in FAR_FIRST]
    for copy in got_a + got_b:
        copy.wait_recv()
    low_half = sa[z]
    high_half = sb[mine]
    for d in range(7):
        low_half = low_half + ra2[d]
        high_half = high_half + rb2[d]

    zcols = pl.ds(pl.multiple_of(z * 128, 128), 128)
    sfull[y, 0:32, zcols] = low_half.astype(BF)
    sfull[y, 32:64, zcols] = high_half.astype(BF)
    got_a, got_b = [], []
    for d in FAR_FIRST:
        got_a.append(start(sfull.at[y, 0:32, zcols], sfull.at[y, 0:32, zcols], at_z(d)))
        got_b.append(start(sfull.at[y, 32:64, zcols], sfull.at[y, 32:64, zcols], at_y(d)))

    part = jnp.concatenate([low_half, high_half], axis=0)
    twice = jnp.concatenate([part, part], axis=0)
    gram = dot_nt(part, twice, HIGHEST)
    gs[...] = jnp.where(lanes((32, 128)) < 64, gram[0:32], gram[32:64])
    got_gram = [start(gs, gr.at[d - 1], at_z(d)) for d in FAR_FIRST]

    for copy in got_a:
        copy.wait_recv()
    spread = [start(sfull.at[y, 0:32], sfull.at[y, 0:32], at_y(d)) for d in FAR_FIRST]
    for copy in got_b:
        copy.wait_recv()
    spread += [start(sfull.at[:, 32:64, zcols], sfull.at[:, 32:64, zcols], at_z(d)) for d in FAR_FIRST]

    blocks = []

    def sum_gram():
        for copy in got_gram + act_came:
            copy.wait_recv()
        total = gs[...]
        for d in range(7):
            total = total + gr[d]
        lane32 = lanes((32, 128))
        rows32 = lax.broadcasted_iota(jnp.int32, (32, 128), 0)
        index = jnp.where(lane32 < 64, rows32, rows32 + 32)
        unused = jnp.where(lane32 % 64 == index, actr[mine, 0:1, :], 0.0)
        blocks.extend(unpack_with_identity(total + unused))

    sum_gram()
    eliminate(blocks, 0, 40)
    for copy in spread:
        copy.wait_recv()

    came = {}
    for q in (2, 1, 3, 0):
        chip = lax.rem(x + q, NX)
        value = dot_nt(sfull[pl.ds(2 * chip, 2)].reshape(128, 1024), lum[...]).astype(BF)
        ut[2 * chip] = value[0:64]
        ut[2 * chip + 1] = value[64:128]
        for par in range(2):
            if (q, par) != (0, 0):
                came[back[(q, par)]] = start(ut.at[res_of(q, par)], utr.at[back[(q, par)]], at_res(q, par))
    utr[0] = ut[r]
    row_cols = pl.ds(pl.multiple_of(y * 128, 128), 128)
    rows_came = []
    for q, par in others:
        rows_came.append(start(sfull.at[res_of(q, par), :, row_cols], srr.at[back[(q, par)]], at_res(q, par)))
    srr[0] = sfull[r, :, row_cols]
    eliminate(blocks, 40, 64)
    linvg[y] = inverse_of(blocks)
    got_inverse = [start(linvg.at[y], linvg.at[y], at_y(d)) for d in FAR_FIRST]

    for slot in range(4):
        if slot:
            came[slot].wait_recv()
        for n in range(4):
            part = dot_nn(utr[slot], wgt[slot, :, 256 * n : 256 * n + 256])
            for t in range(2):
                tile = part[:, 128 * t : 128 * t + 128]
                ia[2 * n + t, 64 * slot : 64 * slot + 64, :] = tile.astype(BF)
    got_a = [start(ia.at[lax.rem(y + d, NY)], ria.at[d - 1], at_y(d)) for d in FAR_FIRST]
    for pair in (1, 0):
        slot = 4 + 2 * pair
        came[slot].wait_recv()
        came[slot + 1].wait_recv()
        for n in range(4):
            cols = slice(256 * n, 256 * n + 256)
            part = jnp.concatenate(
                [dot_nn(utr[slot], wgt[slot, :, cols]), dot_nn(utr[slot + 1], wgt[slot + 1, :, cols])], axis=0
            )
            for t in range(2):
                turned = part[:, 128 * t : 128 * t + 128].T.astype(BF)
                ib[:, 2 * n + t, :, 128 * pair : 128 * pair + 128] = turned.reshape(8, 16, 128)
    got_b = [start(ib.at[lax.rem(z + d, NZ)], rib.at[d - 1], at_z(d)) for d in FAR_FIRST]
    for copy in got_inverse:
        copy.wait_recv()
    inverse_came = []
    for q, par in others:
        inverse_came.append(start(linvg.at[res_of(q, par)], linvr.at[back[(q, par)]], at_res(q, par)))
    linvr[0] = linvg[r]
    for copy in got_a:
        copy.wait_recv()
    total = ia[y].astype(F32)
    for d in range(7):
        total = total + ria[d].astype(F32)
    fa[...] = total.T.reshape(8, 16, 256)
    got_a = [start(fa.at[lax.rem(z + d, NZ)], ria2.at[d - 1], at_z(d)) for d in FAR_FIRST]
    for copy in got_b:
        copy.wait_recv()
    for n in range(8):
        total = ib[z, n].astype(F32)
        for d in range(7):
            total = total + rib[d, n].astype(F32)
        fb[n] = total
    got_b = [start(fb.at[lax.rem(y + d, NY)], rib2.at[d - 1], at_y(d)) for d in FAR_FIRST]

    for copy in rows_came + inverse_came:
        copy.wait_recv()
    both = []
    for t in range(NX):
        factor = block_pair(linvr[2 * t], linvr[2 * t + 1])
        both.append(factor)
        turned = dot_nn(factor, srr[2 * t : 2 * t + 2].reshape(128, 128).astype(F32), HIGHEST).T
        rows[...] = turned.reshape(8, 16, 128)
        value = rows[z]
        basis_ref[res_of(t, 0)] = value[:, 0:64]
        basis_ref[res_of(t, 1)] = pltpu.roll(value, 64, 1)[:, 0:64]
    for copy in got_a + got_b:
        copy.wait_recv()
    first, second = fa[z], fb[y]
    for d in range(7):
        first = first + ria2[d]
        second = second + rib2[d]
    for t in range(NX):
        half = first if t < 2 else second
        value = dot_nt(half[:, 128 * (t % 2) : 128 * (t % 2) + 128], both[t], HIGHEST)
        image_ref[res_of(t, 0)] = value[:, 0:64]
        image_ref[res_of(t, 1)] = pltpu.roll(value, 64, 1)[:, 0:64]
    for copy in pending:
        copy.wait_send()


def local(
    left_u,
    left_v,
    left_rank,
    right_u,
    right_v,
    right_rank,
    near_tiles,
    near_block,
    comp_rank,
    omega,
):
    vmem = pl.BlockSpec(memory_space=pltpu.VMEM)
    smem = pl.BlockSpec(memory_space=pltpu.SMEM)
    scratch = [
        ((4, 64, 1024), BF),
        ((4, 64, 1024), BF),
        ((4, 64, 1024), BF),
        ((4, 64, 1024), BF),
        ((1024, 1024), BF),
        ((64, 1024), BF),
        ((4, 4, 128, 1024), BF),
        ((4, 128, 1024), BF),
        ((256, 1024), BF),
        ((4, 64, 1024), BF),
        ((256, 1024), BF),
        ((8, 64, 256), BF),
        ((8, 64, 256), BF),
        ((8, 32, 1024), BF),
        ((8, 8, 32, 128), BF),
        ((7, 32, 1024), BF),
        ((7, 8, 32, 128), BF),
        ((8, 32, 128), F32),
        ((8, 32, 128), F32),
        ((7, 32, 128), F32),
        ((7, 32, 128), F32),
        ((8, 64, 1024), BF),
        ((32, 128), F32),
        ((7, 32, 128), F32),
        ((8, 32, 128), F32),
        ((8, 32, 128), F32),
        ((8, 64, 128), BF),
        ((8, 64, 256), BF),
        ((8, 64, 256), BF),
        ((512, 1024), BF),
        ((4, 512, 64), BF),
        ((8, 256, 1024), BF),
        ((8, 8, 128), F32),
        ((8, 8, 128), F32),
        ((8, 256, 128), BF),
        ((8, 8, 16, 256), BF),
        ((7, 256, 128), BF),
        ((7, 8, 16, 256), BF),
        ((8, 16, 256), F32),
        ((8, 16, 256), F32),
        ((7, 16, 256), F32),
        ((7, 16, 256), F32),
        ((8, 16, 128), F32),
    ]
    basis, image = pl.pallas_call(
        kernel,
        out_shape=[jax.ShapeDtypeStruct((8, 16, 64), F32)] * 2,
        in_specs=[pl.BlockSpec(memory_space=pl.ANY)] * 6 + [smem] * 4,
        out_specs=[vmem, vmem],
        scratch_shapes=[pltpu.VMEM(shape, dtype) for shape, dtype in scratch]
        + [pltpu.SemaphoreType.DMA((6,)), pltpu.SemaphoreType.DMA((COPIES,)), pltpu.SemaphoreType.DMA((COPIES,))],
        compiler_params=pltpu.CompilerParams(
            collective_id=0, has_side_effects=True, vmem_limit_bytes=60 * 1024 * 1024
        ),
    )(
        jnp.swapaxes(left_v[0], 1, 2),
        jnp.swapaxes(left_u[0], 1, 2),
        jnp.swapaxes(right_u[:, 0], 1, 2),
        jnp.swapaxes(right_v[:, 0], 1, 2),
        near_tiles[0, 0],
        jnp.swapaxes(omega[0], 0, 1),
        left_rank,
        right_rank.T,
        near_block,
        comp_rank.T,
    )
    return basis[:, None], image[:, None]


def solution(mesh):
    placed = (
        P("res", "inner", None, None),
        P("res", "inner", None, None),
        P("res", "inner"),
        P("inner", "res", None, None),
        P("inner", "res", None, None),
        P("inner", "res"),
        P("inner", "res", None, None),
        P("inner", "res"),
        P(None, "res"),
        P("res", None, None),
    )
    return jax.shard_map(
        local,
        mesh=mesh,
        in_specs=placed,
        out_specs=(P(None, "res", "inner", None), P(None, "res", "inner", None)),
        check_vma=False,
    )
```

```python
import jax
import jax.numpy as jnp
from jax import lax
from jax.experimental import pallas as pl
from jax.experimental.pallas import tpu as pltpu
from jax.sharding import PartitionSpec as P

BF = jnp.bfloat16
F32 = jnp.float32
MESH = pl.DeviceIdType.MESH
HIGHEST = lax.Precision.HIGHEST
NY = 8
NZ = 8
NX = 4
FAR_FIRST = (4, 3, 5, 2, 6, 1, 7)
COPIES = 180


def dot_nn(a, b, precision=None):
    return lax.dot_general(a, b, (((1,), (0,)), ((), ())), precision=precision, preferred_element_type=F32)


def dot_nt(a, b, precision=None):
    return lax.dot_general(a, b, (((1,), (1,)), ((), ())), precision=precision, preferred_element_type=F32)


def lanes(shape):
    return lax.broadcasted_iota(jnp.int32, shape, len(shape) - 1)


def row_mask(rank, shape):
    rows = lax.broadcasted_iota(jnp.int32, shape, 0)
    return jnp.where(rows < rank, 1.0, 0.0).astype(BF)


def unpack_with_identity(gram):
    lane32 = lanes((32, 128))
    rows32 = lax.broadcasted_iota(jnp.int32, (32, 128), 0)
    top = jnp.where(lane32 < 64, gram, jnp.where(lane32 - 64 == rows32, 1.0, 0.0))
    bottom = jnp.where(lane32 < 64, pltpu.roll(gram, 64, 1), jnp.where(lane32 - 96 == rows32, 1.0, 0.0))
    return [top[8 * b : 8 * b + 8] for b in range(4)] + [bottom[8 * b : 8 * b + 8] for b in range(4)]


def eliminate(blocks, first, last):
    rows8 = lax.broadcasted_iota(jnp.int32, (8, 128), 0)
    for k in range(first, last):
        kb, kr = k // 8, k % 8
        row = blocks[kb][kr : kr + 1, :]
        scaled = row / row[:, k : k + 1]
        for b in range(kb, 8):
            update = blocks[b][:, k : k + 1] * scaled
            if b == kb:
                update = jnp.where(rows8 > kr, update, 0.0)
            blocks[b] = blocks[b] - update


def inverse_of(blocks):
    lane8 = lanes((8, 128))
    lane32 = lanes((32, 128))
    rows8 = lax.broadcasted_iota(jnp.int32, (8, 128), 0)
    scaled = []
    for b in range(8):
        diagonal = jnp.sum(jnp.where(lane8 == rows8 + 8 * b, blocks[b], 0.0), axis=1, keepdims=True)
        scaled.append(blocks[b] * (1.0 / jnp.sqrt(diagonal)))
    top = jnp.concatenate(scaled[:4], axis=0)
    bottom = jnp.concatenate(scaled[4:], axis=0)
    return jnp.where(lane32 < 64, pltpu.roll(top, 64, 1), bottom)


def block_pair(first, second):
    lane32 = lanes((32, 128))
    left = lane32 < 64
    return jnp.concatenate(
        [
            jnp.where(left, first, 0.0),
            jnp.where(left, pltpu.roll(first, 64, 1), 0.0),
            jnp.where(left, 0.0, pltpu.roll(second, 64, 1)),
            jnp.where(left, 0.0, second),
        ],
        axis=0,
    )


def kernel(
    lv_hbm,
    lu_hbm,
    ru_hbm,
    rv_hbm,
    near_hbm,
    omega_hbm,
    left_rank,
    right_rank,
    near_block,
    comp_rank,
    basis_ref,
    image_ref,
    lv_ref,
    lu_ref,
    ru_ref,
    rv_ref,
    near_ref,
    omega_ref,
    lvb,
    wt,
    lum,
    rum,
    rvm,
    exs,
    exr,
    ska,
    skb,
    ra,
    rb,
    sa,
    sb,
    ra2,
    rb2,
    sfull,
    gs,
    gr,
    linvg,
    linvr,
    srr,
    ut,
    utr,
    lvsel,
    held,
    wgt,
    act,
    actr,
    ia,
    ib,
    ria,
    rib,
    fa,
    fb,
    ria2,
    rib2,
    rows,
    load_sem,
    send_sem,
    recv_sem,
):
    p = lax.axis_index("inner")
    r = lax.axis_index("res")
    y, z = p // NZ, p % NZ
    x, c = r // 2, r % 2
    used = [0]
    moves = (
        (lv_hbm, lv_ref),
        (rv_hbm, rv_ref),
        (omega_hbm, omega_ref),
        (ru_hbm, ru_ref),
        (near_hbm, near_ref),
        (lu_hbm, lu_ref),
    )
    loads = [pltpu.make_async_copy(src, dst, load_sem.at[n]) for n, (src, dst) in enumerate(moves)]
    for load in loads:
        load.start()

    def at_y(d):
        return (lax.rem(y + d, NY) * NZ + z, r)

    def at_z(d):
        return (y * NZ + lax.rem(z + d, NZ), r)

    def at_res(q, par):
        return (p, lax.rem(x + q, NX) * 2 + (c if par == 0 else 1 - c))

    def res_of(q, par):
        return lax.rem(x + q, NX) * 2 + (c if par == 0 else 1 - c)

    def start(src, dst, device):
        n = used[0]
        used[0] += 1
        copy = pltpu.make_async_remote_copy(
            src_ref=src,
            dst_ref=dst,
            send_sem=send_sem.at[n],
            recv_sem=recv_sem.at[n],
            device_id=device,
            device_id_type=MESH,
        )
        copy.start()
        pending.append(copy)
        return copy

    pending = []

    def start_unless_own(distance, src, lands, base, device):
        n = lax.rem(distance + 7, 8)

        @pl.when(distance != 0)
        def _():
            pltpu.make_async_remote_copy(
                src_ref=src,
                dst_ref=lands.at[n],
                send_sem=send_sem.at[base + n],
                recv_sem=recv_sem.at[base + n],
                device_id=device,
                device_id_type=MESH,
            ).start()

    pairs = [(q, par) for q in range(NX) for par in range(2)]
    others = pairs[1:]
    back = {(q, par): ((NX - q) % NX) * 2 + par for q, par in pairs}

    barrier = pltpu.get_barrier_semaphore()
    for d in range(1, NY):
        pl.semaphore_signal(barrier, inc=1, device_id=at_y(d), device_id_type=MESH)
    for d in range(1, NZ):
        pl.semaphore_signal(barrier, inc=1, device_id=at_z(d), device_id_type=MESH)
    for q, par in others:
        pl.semaphore_signal(barrier, inc=1, device_id=at_res(q, par), device_id_type=MESH)

    loads[0].wait()
    for k in range(4):
        lvb[k, 0, 0:64, :] = lv_ref[k] * row_mask(left_rank[0, k], (64, 1024))
    pl.semaphore_wait(barrier, NY - 1 + NZ - 1 + 7)

    nb = near_block[0, 0]

    def pick_near(q):
        rows = slice(128 * q, 128 * q + 128)
        kept = jnp.zeros((128, 1024), BF)
        for k in range(4):
            kept = jnp.where(nb == k, lvb[k, q], kept)
            held[k, rows, :] = dot_nt(lvb[k, q], rum[k]).astype(BF)
        lvsel[rows, :] = kept

    def make_weights(n):
        cols = slice(256 * n, 256 * n + 256)
        tile = near_ref[:, cols]
        for q in range(NX):
            rows = slice(128 * q, 128 * q + 128)
            near_part = dot_nn(lvsel[rows, :], tile)
            for k in range(4):
                far_part = dot_nn(held[k, rows, :], rvm[64 * k : 64 * k + 64, cols])
                value = jnp.where(nb == k, near_part, far_part).astype(BF)
                wgt[2 * q, 64 * k : 64 * k + 64, cols] = value[0:64]
                wgt[2 * q + 1, 64 * k : 64 * k + 64, cols] = value[64:128]

    def piece_of(step, n):
        return lambda: step(n)

    weight_work = [piece_of(pick_near, q) for q in range(4)] + [piece_of(make_weights, n) for n in range(4)]

    sibling = at_res(0, 1)
    sib_own = start(lvb.at[:, 0, 0:64], lvb.at[:, 0, 64:128], sibling)
    came_v = {}
    for k in range(4):
        turned = (k + 2) % 4
        came_v[3, k] = start(lvb.at[k, 0, 0:64], lvb.at[k, 3, 0:64], at_res(1, 0))
        came_v[1, turned] = start(lvb.at[turned, 0, 0:64], lvb.at[turned, 1, 0:64], at_res(3, 0))

    fwd = {1: [], 2: [], 3: []}

    def forward(q, k):
        came_v[q, k].wait_recv()
        if (q, k) in ((3, 0), (3, 1)):
            came_v[2, k] = start(lvb.at[k, 3, 0:64], lvb.at[k, 2, 0:64], at_res(1, 0))
        if (q, k) in ((1, 2), (1, 3)):
            came_v[2, k] = start(lvb.at[k, 1, 0:64], lvb.at[k, 2, 0:64], at_res(3, 0))
        fwd[q].append(start(lvb.at[k, q, 0:64], lvb.at[k, q, 64:128], sibling))

    act_came = []
    for q, par in pairs:
        lane8 = lanes((8, 128)) % 64
        unused = jnp.where(lane8 < comp_rank[0, res_of(q, par)], 0.0, 1.0)
        if (q, par) == (0, 0):
            actr[0] = unused
        else:
            act[2 * q + par] = unused
            act_came.append(start(act.at[2 * q + par], actr.at[back[(q, par)]], at_res(q, par)))

    for load in loads[1:]:
        load.wait()
    for k in range(4):
        mask = row_mask(right_rank[0, k], (64, 1024))
        rum[k] = ru_ref[k] * mask
        rvm[64 * k : 64 * k + 64, :] = rv_ref[k] * mask
        lum[64 * k : 64 * k + 64, :] = lu_ref[k] * row_mask(left_rank[0, k], (64, 1024))
    omega = omega_ref[...]
    mixed = [dot_nt(omega, rvm[64 * k : 64 * k + 64, :]) for k in range(4)]
    for n in range(4):
        cols = slice(256 * n, 256 * n + 256)
        near_omega = dot_nt(omega, near_ref[cols, :])
        for k in range(4):
            high = mixed[k].astype(BF)
            low = (mixed[k] - high.astype(F32)).astype(BF)
            part = dot_nn(high, rum[k, :, cols]) + dot_nn(low, rum[k, :, cols])
            full = jnp.where(nb == k, near_omega, part)
            high = full.astype(BF)
            wt[k, 0:64, cols] = high
            wt[k, 64:128, cols] = (full - high.astype(F32)).astype(BF)
        if n % 2:
            forward(3, n // 2)
            forward(1, n // 2 + 2)

    def expand_chip(q):
        lane = lanes((64, 128))
        parts = []
        for k in range(4):
            both = dot_nt(wt[k], lvb[k, q])
            parts.append(both[0:64] + both[64:128])
        rolled = [pltpu.roll(part, 64, 1) for part in parts]
        for par in range(2):
            if par == 0:
                tiles = [jnp.where(lane < 64, parts[2 * t], rolled[2 * t + 1]) for t in range(2)]
            else:
                tiles = [jnp.where(lane < 64, rolled[2 * t], parts[2 * t + 1]) for t in range(2)]
            active = row_mask(comp_rank[0, res_of(q, par)], (64, 128))
            for t in range(2):
                value = tiles[t].astype(BF) * active
                if (q, par) == (0, 0):
                    exr[0, :, 128 * t : 128 * t + 128] = value
                else:
                    exs[2 * q + par, :, 128 * t : 128 * t + 128] = value

    came = {}

    def send_expand(q, par):
        slot = back[(q, par)]
        came[slot] = start(exs.at[2 * q + par], exr.at[slot], at_res(q, par))

    sib_own.wait_recv()
    expand_chip(0)
    send_expand(0, 1)

    def expand_and_send(q):
        for copy in fwd[q]:
            copy.wait_recv()
        expand_chip(q)
        send_expand(q, 0)
        send_expand(q, 1)

    def slot_of(column):
        return lax.rem(column // 2 - x + NX, NX) * 2 + lax.rem(column + c, 2)

    place = {0: 0, 3: 1, 1: 2, 2: 3}

    def sketch_chip(q):
        for par in range(2):
            if (q, par) != (0, 0):
                came[2 * q + par].wait_recv()
        factor = exr[2 * q : 2 * q + 2].reshape(128, 256)
        for n in range(4):
            part = dot_nn(factor, lum[:, 256 * n : 256 * n + 256]).astype(BF)
            for par in range(2):
                ska[2 * q + par, :, 256 * n : 256 * n + 256] = part[64 * par : 64 * par + 32]
                for t in range(2):
                    tile = part[64 * par + 32 : 64 * par + 64, 128 * t : 128 * t + 128]
                    skb[2 * n + t, 2 * place[q] + par] = tile
        for par in range(2):
            column = res_of(q, par)
            distance = lax.rem(column - y + NY, NY)
            start_unless_own(distance, ska.at[2 * q + par], ra, sums_base, (column * NZ + z, r))

    got_b = []

    def send_high(tiles):
        for d in FAR_FIRST:
            got_b.append(start(skb.at[lax.rem(z + d, NZ), tiles], rb.at[d - 1, tiles], at_z(d)))

    sums_base = used[0]
    used[0] += 7
    got_a = []
    for d in range(7):
        got_a.append(
            pltpu.make_async_remote_copy(
                src_ref=ska.at[0],
                dst_ref=ra.at[d],
                send_sem=send_sem.at[sums_base + d],
                recv_sem=recv_sem.at[sums_base + d],
                device_id=at_y(d + 1),
                device_id_type=MESH,
            )
        )
    pending.extend(got_a)
    for k in (2, 3):
        forward(3, k)
        forward(1, k - 2)
    expand_and_send(3)
    expand_and_send(1)
    sketch_chip(0)
    send_high(slice(0, 2))
    for k in (0, 2, 1, 3):
        forward(2, k)
    expand_and_send(2)
    sketch_chip(3)
    sketch_chip(1)
    send_high(slice(2, 6))
    sketch_chip(2)
    send_high(slice(6, 8))
    for piece in weight_work:
        piece()
    for copy in got_a:
        copy.wait_recv()
    mine = slot_of(y)
    for n in range(8):
        cols = slice(128 * n, 128 * n + 128)
        total = ska[mine, :, cols].astype(F32)
        for d in range(7):
            total = total + ra[d, :, cols].astype(F32)
        sa[n] = total
    got_a = [start(sa.at[lax.rem(z + d, NZ)], ra2.at[d - 1], at_z(d)) for d in FAR_FIRST]
    for copy in got_b:
        copy.wait_recv()
    for q, par in pairs:
        n = 2 * place[q] + par
        total = skb[z, n].astype(F32)
        for d in range(7):
            total = total + rb[d, n].astype(F32)
        sb[2 * q + par] = total
    got_b = [start(sb.at[slot_of(lax.rem(y + d, NY))], rb2.at[d - 1], at_y(d)) for d in FAR_FIRST]
    for copy in got_a + got_b:
        copy.wait_recv()
    low_half = sa[z]
    high_half = sb[mine]
    for d in range(7):
        low_half = low_half + ra2[d]
        high_half = high_half + rb2[d]

    zcols = pl.ds(pl.multiple_of(z * 128, 128), 128)
    sfull[y, 0:32, zcols] = low_half.astype(BF)
    sfull[y, 32:64, zcols] = high_half.astype(BF)
    got_a, got_b = [], []
    for d in FAR_FIRST:
        got_a.append(start(sfull.at[y, 0:32, zcols], sfull.at[y, 0:32, zcols], at_z(d)))
        got_b.append(start(sfull.at[y, 32:64, zcols], sfull.at[y, 32:64, zcols], at_y(d)))

    part = jnp.concatenate([low_half, high_half], axis=0)
    twice = jnp.concatenate([part, part], axis=0)
    gram = dot_nt(part, twice, HIGHEST)
    gs[...] = jnp.where(lanes((32, 128)) < 64, gram[0:32], gram[32:64])
    got_gram = [start(gs, gr.at[d - 1], at_z(d)) for d in FAR_FIRST]

    for copy in got_a:
        copy.wait_recv()
    spread = [start(sfull.at[y, 0:32], sfull.at[y, 0:32], at_y(d)) for d in FAR_FIRST]
    for copy in got_b:
        copy.wait_recv()
    spread += [start(sfull.at[:, 32:64, zcols], sfull.at[:, 32:64, zcols], at_z(d)) for d in FAR_FIRST]

    blocks = []

    def sum_gram():
        for copy in got_gram + act_came:
            copy.wait_recv()
        total = gs[...]
        for d in range(7):
            total = total + gr[d]
        lane32 = lanes((32, 128))
        rows32 = lax.broadcasted_iota(jnp.int32, (32, 128), 0)
        index = jnp.where(lane32 < 64, rows32, rows32 + 32)
        unused = jnp.where(lane32 % 64 == index, actr[mine, 0:1, :], 0.0)
        blocks.extend(unpack_with_identity(total + unused))

    sum_gram()
    eliminate(blocks, 0, 40)
    for copy in spread:
        copy.wait_recv()

    came = {}
    for q in (2, 1, 3, 0):
        chip = lax.rem(x + q, NX)
        value = dot_nt(sfull[pl.ds(2 * chip, 2)].reshape(128, 1024), lum[...]).astype(BF)
        ut[2 * chip] = value[0:64]
        ut[2 * chip + 1] = value[64:128]
        for par in range(2):
            if (q, par) != (0, 0):
                came[back[(q, par)]] = start(ut.at[res_of(q, par)], utr.at[back[(q, par)]], at_res(q, par))
    utr[0] = ut[r]
    row_cols = pl.ds(pl.multiple_of(y * 128, 128), 128)
    rows_came = []
    for q, par in others:
        rows_came.append(start(sfull.at[res_of(q, par), :, row_cols], srr.at[back[(q, par)]], at_res(q, par)))
    srr[0] = sfull[r, :, row_cols]
    eliminate(blocks, 40, 64)
    linvg[y] = inverse_of(blocks)
    got_inverse = [start(linvg.at[y], linvg.at[y], at_y(d)) for d in FAR_FIRST]

    for slot in range(4):
        if slot:
            came[slot].wait_recv()
        for n in range(4):
            part = dot_nn(utr[slot], wgt[slot, :, 256 * n : 256 * n + 256])
            for t in range(2):
                tile = part[:, 128 * t : 128 * t + 128]
                ia[2 * n + t, 64 * slot : 64 * slot + 64, :] = tile.astype(BF)
    got_a = [start(ia.at[lax.rem(y + d, NY)], ria.at[d - 1], at_y(d)) for d in FAR_FIRST]
    for pair in (1, 0):
        slot = 4 + 2 * pair
        came[slot].wait_recv()
        came[slot + 1].wait_recv()
        for n in range(4):
            cols = slice(256 * n, 256 * n + 256)
            part = jnp.concatenate(
                [dot_nn(utr[slot], wgt[slot, :, cols]), dot_nn(utr[slot + 1], wgt[slot + 1, :, cols])], axis=0
            )
            for t in range(2):
                turned = part[:, 128 * t : 128 * t + 128].T.astype(BF)
                ib[:, 2 * n + t, :, 128 * pair : 128 * pair + 128] = turned.reshape(8, 16, 128)
    got_b = [start(ib.at[lax.rem(z + d, NZ)], rib.at[d - 1], at_z(d)) for d in FAR_FIRST]
    for copy in got_inverse:
        copy.wait_recv()
    inverse_came = []
    for q, par in others:
        inverse_came.append(start(linvg.at[res_of(q, par)], linvr.at[back[(q, par)]], at_res(q, par)))
    linvr[0] = linvg[r]
    for copy in got_a:
        copy.wait_recv()
    total = ia[y].astype(F32)
    for d in range(7):
        total = total + ria[d].astype(F32)
    fa[...] = total.T.reshape(8, 16, 256)
    got_a = [start(fa.at[lax.rem(z + d, NZ)], ria2.at[d - 1], at_z(d)) for d in FAR_FIRST]
    for copy in got_b:
        copy.wait_recv()
    for n in range(8):
        total = ib[z, n].astype(F32)
        for d in range(7):
            total = total + rib[d, n].astype(F32)
        fb[n] = total
    got_b = [start(fb.at[lax.rem(y + d, NY)], rib2.at[d - 1], at_y(d)) for d in FAR_FIRST]

    for copy in rows_came + inverse_came:
        copy.wait_recv()
    both = []
    for t in range(NX):
        factor = block_pair(linvr[2 * t], linvr[2 * t + 1])
        both.append(factor)
        turned = dot_nn(factor, srr[2 * t : 2 * t + 2].reshape(128, 128).astype(F32), HIGHEST).T
        rows[...] = turned.reshape(8, 16, 128)
        value = rows[z]
        basis_ref[res_of(t, 0)] = value[:, 0:64]
        basis_ref[res_of(t, 1)] = pltpu.roll(value, 64, 1)[:, 0:64]
    for copy in got_a + got_b:
        copy.wait_recv()
    first, second = fa[z], fb[y]
    for d in range(7):
        first = first + ria2[d]
        second = second + rib2[d]
    for t in range(NX):
        half = first if t < 2 else second
        value = dot_nt(half[:, 128 * (t % 2) : 128 * (t % 2) + 128], both[t], HIGHEST)
        image_ref[res_of(t, 0)] = value[:, 0:64]
        image_ref[res_of(t, 1)] = pltpu.roll(value, 64, 1)[:, 0:64]
    for copy in pending:
        copy.wait_send()


def local(
    left_u,
    left_v,
    left_rank,
    right_u,
    right_v,
    right_rank,
    near_tiles,
    near_block,
    comp_rank,
    omega,
):
    vmem = pl.BlockSpec(memory_space=pltpu.VMEM)
    smem = pl.BlockSpec(memory_space=pltpu.SMEM)
    scratch = [
        ((4, 64, 1024), BF),
        ((4, 64, 1024), BF),
        ((4, 64, 1024), BF),
        ((4, 64, 1024), BF),
        ((1024, 1024), BF),
        ((64, 1024), BF),
        ((4, 4, 128, 1024), BF),
        ((4, 128, 1024), BF),
        ((256, 1024), BF),
        ((4, 64, 1024), BF),
        ((256, 1024), BF),
        ((8, 64, 256), BF),
        ((8, 64, 256), BF),
        ((8, 32, 1024), BF),
        ((8, 8, 32, 128), BF),
        ((7, 32, 1024), BF),
        ((7, 8, 32, 128), BF),
        ((8, 32, 128), F32),
        ((8, 32, 128), F32),
        ((7, 32, 128), F32),
        ((7, 32, 128), F32),
        ((8, 64, 1024), BF),
        ((32, 128), F32),
        ((7, 32, 128), F32),
        ((8, 32, 128), F32),
        ((8, 32, 128), F32),
        ((8, 64, 128), BF),
        ((8, 64, 256), BF),
        ((8, 64, 256), BF),
        ((512, 1024), BF),
        ((4, 512, 64), BF),
        ((8, 256, 1024), BF),
        ((8, 8, 128), F32),
        ((8, 8, 128), F32),
        ((8, 256, 128), BF),
        ((8, 8, 16, 256), BF),
        ((7, 256, 128), BF),
        ((7, 8, 16, 256), BF),
        ((8, 16, 256), F32),
        ((8, 16, 256), F32),
        ((7, 16, 256), F32),
        ((7, 16, 256), F32),
        ((8, 16, 128), F32),
    ]
    basis, image = pl.pallas_call(
        kernel,
        out_shape=[jax.ShapeDtypeStruct((8, 16, 64), F32)] * 2,
        in_specs=[pl.BlockSpec(memory_space=pl.ANY)] * 6 + [smem] * 4,
        out_specs=[vmem, vmem],
        scratch_shapes=[pltpu.VMEM(shape, dtype) for shape, dtype in scratch]
        + [pltpu.SemaphoreType.DMA((6,)), pltpu.SemaphoreType.DMA((COPIES,)), pltpu.SemaphoreType.DMA((COPIES,))],
        compiler_params=pltpu.CompilerParams(
            collective_id=0, has_side_effects=True, vmem_limit_bytes=60 * 1024 * 1024
        ),
    )(
        jnp.swapaxes(left_v[0], 1, 2),
        jnp.swapaxes(left_u[0], 1, 2),
        jnp.swapaxes(right_u[:, 0], 1, 2),
        jnp.swapaxes(right_v[:, 0], 1, 2),
        near_tiles[0, 0],
        jnp.swapaxes(omega[0], 0, 1),
        left_rank,
        right_rank.T,
        near_block,
        comp_rank.T,
    )
    return basis[:, None], image[:, None]


def solution(mesh):
    placed = (
        P("res", "inner", None, None),
        P("res", "inner", None, None),
        P("res", "inner"),
        P("inner", "res", None, None),
        P("inner", "res", None, None),
        P("inner", "res"),
        P("inner", "res", None, None),
        P("inner", "res"),
        P(None, "res"),
        P("res", None, None),
    )
    return jax.shard_map(
        local,
        mesh=mesh,
        in_specs=placed,
        out_specs=(P(None, "res", "inner", None), P(None, "res", "inner", None)),
        check_vma=False,
    )
```
